32 devices in a mesh: fsdp: 4 (over y, x), seq: 8 (over z, core).
Axes of the slice: x: 2, y: 2, z: 4, core: 2. Of those that a mesh axis runs over, the one named last changes fastest.
Arguments:
- tokens: bfloat16 [4, 2048, 4096], P('fsdp', 'seq'), may hold values from -6 to 6
- queries: bfloat16 [4, 2048, 4096], P('fsdp', 'seq'), may hold values from -70 to 70
- key_weight: bfloat16 [4096, 1024], P(('fsdp', 'seq')), may hold values from -0.09375 to 0.09375
- value_weight: bfloat16 [4096, 1024], P(('fsdp', 'seq')), may hold values from -0.09375 to 0.09375
- sorted_blocks: int32 [4, 8, 16], P('fsdp', None, 'seq'), may hold values from 0 to 15, as said below
Outputs:
- attended: bfloat16 [4, 2048, 4096], P('fsdp', 'seq')
The draws below stay inside these ranges and needn't reach their ends.
Inputs may be any that keep to these rules, and one draw needn't show every extreme that they name: `sorted_blocks`: for each sequence and key-value head, a permutation of the 16 blocks. The 2 blocks of one device, over all key-value heads, name blocks that lie on one device at most 2 times, and for one head at most 1 times; both bounds are reached in every draw. Device d holds blocks d * 2 to d * 2 + 1.
All inputs are finite; a program needn't handle non-finite values.
Results may differ from the reference program's by a relative error of at most 0.012.
The reference program's roundings to bfloat16 on the way count: a program that leaves them out, or rounds other values in their place, can miss the bound.
Values may be sent and summed in bfloat16 or wider, within the bound.
No kernel may reach another device: no remote copies, remote signals or barrier semaphores. Data moves between devices by JAX's collectives and lax.ppermute only.
A program may use at most 128 MiB of HBM per device.

```python
import math
import jax
import jax.numpy as jnp
from jax import lax

D = 4096
DH = 128
KVH = 8
GROUP = 4
BLOCK = 128
BLK_DEV = 2
NB = 16
L = 2048
SEQS = 4


def draw_queries(key, part):
    first_key = jax.random.fold_in(jax.random.fold_in(key, 11), 0)
    values_out = jnp.clip(jax.random.normal(first_key, (SEQS, L, KVH * GROUP * DH), jnp.float32), -6.0, 6.0)
    return values_out.astype(jnp.bfloat16)


def one_sequence(seq_key):
    devices = NB // BLK_DEV
    first_key, second_key, third_key = jax.random.split(seq_key, 3)
    relabel = jax.random.permutation(first_key, devices)
    inverse = jnp.argsort(relabel)
    shifts = jax.random.permutation(second_key, devices)[jnp.arange(KVH * BLK_DEV) % devices].reshape(KVH, BLK_DEV)
    slot_perm = jax.vmap(lambda slot_key: jax.random.permutation(slot_key, BLK_DEV))(jax.random.split(third_key, KVH))
    target = relabel[(inverse[None, :, None] + shifts[:, None, :]) % devices]
    return (target * BLK_DEV + slot_perm[:, None, :]).reshape(KVH, NB).astype(jnp.int32)


def draw_sorted_blocks(key, part):
    base_key = jax.random.fold_in(key, 23)
    seq_keys = jax.vmap(lambda index: jax.random.fold_in(base_key, index))(jnp.arange(SEQS))
    return jax.vmap(one_sequence)(seq_keys)


def block_levels(key, shape, shards, least, top_value):
    gain = 1.0
    for position, parts in shards:
        heights = jax.random.uniform(jax.random.fold_in(jax.random.fold_in(key, 6), position), (parts,), jnp.float32, least / len(shards), top_value / len(shards))
        gain = gain * jnp.repeat(jnp.exp(heights), shape[position] // parts).reshape((-1,) + (1,) * (len(shape) - 1 - position))
    return gain


def gaussian(own_key, dims, deviation, reach, pieces=(), kind=jnp.bfloat16):
    drawn = jax.random.normal(own_key, dims, jnp.float32) * deviation
    if len(pieces) > 0:
        drawn = block_levels(own_key, dims, pieces, -0.22, 0.18) * drawn
    return jnp.clip(drawn, min=-reach, max=reach).astype(kind)


def setup_inputs(seed: int = 0) -> dict:
    streams_of = jax.random.split(jax.random.key(seed), 6)
    return {
        "tokens": gaussian(streams_of[0], (SEQS, L, D), 1.0, 6.0, ((0, 4), (1, 8))),
        "queries": draw_queries(jax.random.fold_in(streams_of[5], 71), 0),
        "key_weight": gaussian(streams_of[2], (D, KVH * DH), D ** -0.5, 0.09375, ((0, 32),)),
        "value_weight": gaussian(streams_of[3], (D, KVH * DH), D ** -0.5, 0.09375, ((0, 32),)),
        "sorted_blocks": draw_sorted_blocks(jax.random.fold_in(streams_of[5], 71), 0),
    }


def attend_head(query_head, candidate_head):
    key_part = candidate_head[:, :, :DH].astype(jnp.float32)
    value_part = candidate_head[:, :, DH:].astype(jnp.float32)
    scores = jnp.einsum('btge,bke->gbtk', query_head.astype(jnp.float32), key_part) * (1.0 / math.sqrt(DH))
    block_index = jnp.arange(NB, dtype=jnp.int32)
    key_index = jnp.arange(3 * BLOCK, dtype=jnp.int32)
    blocked = (block_index[:, None] == 0) & (key_index[None, :] >= BLOCK) & (key_index[None, :] < 2 * BLOCK)
    scores = jnp.where(blocked[None, :, None, :], -1e+30, scores)
    highest = lax.optimization_barrier(jnp.max(scores, axis=-1, keepdims=True))
    raised = jnp.exp(scores - highest)
    weights = (raised / lax.optimization_barrier(jnp.sum(raised, axis=-1, keepdims=True))).astype(jnp.bfloat16)
    result = jnp.einsum('gbtk,bke->btge', weights.astype(jnp.float32), value_part)
    return result.astype(jnp.bfloat16)

def pick_blocks(kv_table, wanted):
    return jnp.take(kv_table, wanted, axis=0)

def run_head(inputs):
    return attend_head(inputs[0], inputs[1])

def reference(tokens, queries, key_weight, value_weight, sorted_blocks):
    outputs = []
    for sequence in range(SEQS):
        key_all = jnp.dot(tokens[sequence], key_weight, preferred_element_type=jnp.float32).astype(jnp.bfloat16)
        value_all = jnp.dot(tokens[sequence], value_weight, preferred_element_type=jnp.float32).astype(jnp.bfloat16)
        key_blocks = key_all.reshape(NB, BLOCK, KVH, DH)
        value_blocks = value_all.reshape(NB, BLOCK, KVH, DH)
        packed = jnp.concatenate([key_blocks, value_blocks], axis=3).transpose(2, 0, 1, 3)
        preceding = jnp.concatenate([jnp.zeros_like(packed[:, :1]), packed[:, :NB - 1]], axis=1)
        chosen = jax.vmap(pick_blocks)(packed, sorted_blocks[sequence].astype(jnp.int32))
        candidates = jnp.concatenate([packed, preceding, chosen], axis=2)
        query_heads = queries[sequence].reshape(NB, BLOCK, KVH, GROUP, DH).transpose(2, 0, 1, 3, 4)
        results = lax.map(run_head, (query_heads, candidates))
        outputs.append(results.transpose(1, 2, 0, 3, 4).reshape(L, KVH * GROUP * DH))
    return jnp.stack(outputs)
```

```python
import functools
import math

import jax
import jax.numpy as jnp
from jax import lax
from jax.experimental import pallas as pl
from jax.experimental.pallas import tpu as pltpu
from jax.sharding import PartitionSpec as P

DH = 128
KVH = 8
GROUP = 4
BLOCK = 128
EXP2_SCALE = math.log2(math.e) / math.sqrt(DH)


def plan_sends(all_targets, me, local_blocks, capacity):
    devices = all_targets.shape[0]
    targets = all_targets.reshape(devices, -1)
    heads = jnp.arange(targets.shape[1], dtype=jnp.int32) // local_blocks
    mine = targets // local_blocks == me
    rank = jnp.cumsum(mine.astype(jnp.int32), axis=1) - 1
    row = heads[None, :] * local_blocks + targets % local_blocks
    hit = mine[:, :, None] & (rank[:, :, None] == jnp.arange(capacity, dtype=jnp.int32))
    return jnp.sum(jnp.where(hit, row[:, :, None], 0), axis=1)


def plan_receives(targets, local_blocks, capacity):
    owner = targets.reshape(-1) // local_blocks
    order = jnp.arange(owner.shape[0], dtype=jnp.int32)
    same = (owner[:, None] == owner[None, :]) & (order[None, :] < order[:, None])
    return owner * capacity + jnp.sum(same.astype(jnp.int32), axis=1)


def attend_kernel(place_ref, first_ref, q_ref, k_ref, v_ref, pk_ref, pv_ref, *rest):
    sorted_refs, out_ref = rest[:-1], rest[-1]
    blocks = k_ref.shape[0] // BLOCK
    for b in range(blocks):
        rows = pl.ds(b * BLOCK, BLOCK)
        before = pl.ds((b - 1) * BLOCK, BLOCK)
        k_prev = pk_ref[...] if b == 0 else k_ref[before, :]
        v_prev = pv_ref[...] if b == 0 else v_ref[before, :]
        sorted_kv = sorted_refs[b][0]
        keys = jnp.concatenate([k_ref[rows, :], k_prev, sorted_kv[:, :DH]], axis=0)
        values = jnp.concatenate([v_ref[rows, :], v_prev, sorted_kv[:, DH:]], axis=0)
        q = jnp.concatenate([q_ref[rows, pl.ds(g * DH, DH)] for g in range(GROUP)], axis=0)
        scores = lax.dot_general(q, keys, (((1,), (1,)), ((), ())), preferred_element_type=jnp.float32)
        if b == 0:
            column = lax.broadcasted_iota(jnp.int32, (1, 3 * BLOCK), 1)
            blocked = (column >= BLOCK) & (column < 2 * BLOCK) & (first_ref[0] == 1)
            scores = jnp.where(blocked, -1e30, scores)
        raised = jnp.exp2((scores - jnp.max(scores, axis=-1, keepdims=True)) * EXP2_SCALE)
        weights = (raised * (1.0 / jnp.sum(raised, axis=-1, keepdims=True))).astype(jnp.bfloat16)
        result = jnp.dot(weights, values, preferred_element_type=jnp.float32).astype(jnp.bfloat16)
        for g in range(GROUP):
            out_ref[rows, pl.ds(g * DH, DH)] = result[g * BLOCK : (g + 1) * BLOCK]


def attend(place, first, queries, keys, values, prev_keys, prev_values, arrived):
    tokens = queries.shape[0]
    blocks = tokens // BLOCK
    head_columns = lambda h, place, first: (0, h)
    sorted_specs = [
        pl.BlockSpec((1, BLOCK, 2 * DH), lambda h, place, first, b=b: (place[h * blocks + b], 0, 0))
        for b in range(blocks)
    ]
    return pl.pallas_call(
        attend_kernel,
        grid_spec=pltpu.PrefetchScalarGridSpec(
            num_scalar_prefetch=2,
            grid=(KVH,),
            in_specs=[
                pl.BlockSpec((tokens, GROUP * DH), head_columns),
                pl.BlockSpec((tokens, DH), head_columns),
                pl.BlockSpec((tokens, DH), head_columns),
                pl.BlockSpec((BLOCK, DH), head_columns),
                pl.BlockSpec((BLOCK, DH), head_columns),
                *sorted_specs,
            ],
            out_specs=pl.BlockSpec((tokens, GROUP * DH), head_columns),
        ),
        out_shape=jax.ShapeDtypeStruct(queries.shape, jnp.bfloat16),
        compiler_params=pltpu.CompilerParams(vmem_limit_bytes=32 * 1024 * 1024),
    )(place, first, queries, keys, values, prev_keys, prev_values, *([arrived] * blocks))


def project(token_rows, key_weight, value_weight):
    weights = lax.all_gather(
        jnp.concatenate([key_weight, value_weight], axis=1), ("fsdp", "seq"), axis=0, tiled=True
    )
    packed = jnp.dot(token_rows, weights, preferred_element_type=jnp.float32).astype(jnp.bfloat16)
    return packed[:, : KVH * DH], packed[:, KVH * DH :]


def local(tokens, queries, key_weight, value_weight, sorted_blocks):
    local_blocks = tokens.shape[1] // BLOCK
    devices = lax.axis_size("seq")
    me = lax.axis_index("seq")
    capacity = (KVH * local_blocks + devices - 1) // devices
    targets = sorted_blocks[0]
    wanted = plan_sends(lax.all_gather(targets, "seq", axis=0), me, local_blocks, capacity)
    place = plan_receives(targets, local_blocks, capacity)

    keys, values = project(tokens[0], key_weight, value_weight)
    edge = jnp.concatenate([keys[-BLOCK:], values[-BLOCK:]], axis=1)
    prev = lax.ppermute(edge, "seq", [(i, i + 1) for i in range(devices - 1)])

    def table(rows):
        return rows.reshape(local_blocks, BLOCK, KVH, DH).transpose(2, 0, 1, 3)

    packed = jnp.concatenate([table(keys), table(values)], axis=3).reshape(-1, BLOCK, 2 * DH)
    replies = jnp.take(packed, wanted.reshape(-1), axis=0)
    arrived = lax.all_to_all(replies, "seq", split_axis=0, concat_axis=0, tiled=True)
    first = (me == 0).astype(jnp.int32).reshape(1)
    out = attend(place, first, queries[0], keys, values, prev[:, : KVH * DH], prev[:, KVH * DH :], arrived)
    return out[None]


def solution(mesh):
    placed = (
        P("fsdp", "seq", None),
        P("fsdp", "seq", None),
        P(("fsdp", "seq"), None),
        P(("fsdp", "seq"), None),
        P("fsdp", None, "seq"),
    )
    return jax.shard_map(
        local, mesh=mesh, in_specs=placed, out_specs=P("fsdp", "seq", None), check_vma=False
    )
```

```python
import functools
import math

import jax
import jax.numpy as jnp
from jax import lax
from jax.experimental import pallas as pl
from jax.experimental.pallas import tpu as pltpu
from jax.sharding import Mesh, PartitionSpec as P

DH = 128
KVH = 8
GROUP = 4
BLOCK = 128
EXP2_SCALE = math.log2(math.e) / math.sqrt(DH)


def plan_sends(all_targets, me, local_blocks, capacity):
    devices = all_targets.shape[0]
    targets = all_targets.reshape(devices, -1)
    heads = jnp.arange(targets.shape[1], dtype=jnp.int32) // local_blocks
    mine = targets // local_blocks == me
    rank = jnp.cumsum(mine.astype(jnp.int32), axis=1) - 1
    row = heads[None, :] * local_blocks + targets % local_blocks
    hit = mine[:, :, None] & (rank[:, :, None] == jnp.arange(capacity, dtype=jnp.int32))
    return jnp.sum(jnp.where(hit, row[:, :, None], 0), axis=1)


def plan_receives(targets, local_blocks, capacity):
    owner = targets.reshape(-1) // local_blocks
    order = jnp.arange(owner.shape[0], dtype=jnp.int32)
    same = (owner[:, None] == owner[None, :]) & (order[None, :] < order[:, None])
    return owner * capacity + jnp.sum(same.astype(jnp.int32), axis=1)


def attend_kernel(place_ref, where_ref, q_ref, k_ref, v_ref, pk_ref, pv_ref, *rest):
    sorted_refs, out_ref = rest[:-1], rest[-1]
    k_ref, v_ref, pk_ref, pv_ref = [ref.at[0, 0] for ref in (k_ref, v_ref, pk_ref, pv_ref)]
    blocks = k_ref.shape[0] // BLOCK
    for b in range(blocks):
        rows = pl.ds(b * BLOCK, BLOCK)
        before = pl.ds((b - 1) * BLOCK, BLOCK)
        k_prev = pk_ref[...] if b == 0 else k_ref[before, :]
        v_prev = pv_ref[...] if b == 0 else v_ref[before, :]
        keys = jnp.concatenate([k_ref[rows, :], k_prev, sorted_refs[2 * b][0, 0]], axis=0)
        values = jnp.concatenate([v_ref[rows, :], v_prev, sorted_refs[2 * b + 1][0, 0]], axis=0)
        q = jnp.concatenate([q_ref[rows, pl.ds(g * DH, DH)] for g in range(GROUP)], axis=0)
        scores = lax.dot_general(q, keys, (((1,), (1,)), ((), ())), preferred_element_type=jnp.float32)
        if b == 0:
            column = lax.broadcasted_iota(jnp.int32, (1, 3 * BLOCK), 1)
            blocked = (column >= BLOCK) & (column < 2 * BLOCK) & (where_ref[0] == 1)
            scores = jnp.where(blocked, -1e30, scores)
        raised = jnp.exp2((scores - jnp.max(scores, axis=-1, keepdims=True)) * EXP2_SCALE)
        weights = (raised * (1.0 / jnp.sum(raised, axis=-1, keepdims=True))).astype(jnp.bfloat16)
        result = jnp.dot(weights, values, preferred_element_type=jnp.float32).astype(jnp.bfloat16)
        for g in range(GROUP):
            out_ref[rows, pl.ds(g * DH, DH)] = result[g * BLOCK : (g + 1) * BLOCK]


def attend(place, where, queries, own, prev, arrived):
    tokens = queries.shape[0]
    blocks = tokens // BLOCK
    heads = own.shape[3] // DH

    def kv_spec(rows, kind, at):
        def index(h, place, where):
            return (where[1] ^ kind, (h // heads) ^ where[at], 0, h % heads)

        return pl.BlockSpec((1, 1, rows, DH), index)

    def sorted_spec(b, kind):
        return pl.BlockSpec((1, 1, BLOCK, DH), lambda h, place, where: (kind, place[h * blocks + b], 0, 0))

    q_spec = pl.BlockSpec((tokens, GROUP * DH), lambda h, place, where: (0, h))
    return pl.pallas_call(
        attend_kernel,
        grid_spec=pltpu.PrefetchScalarGridSpec(
            num_scalar_prefetch=2,
            grid=(KVH,),
            in_specs=[
                q_spec,
                kv_spec(tokens, 0, 2),
                kv_spec(tokens, 1, 2),
                kv_spec(BLOCK, 0, 3),
                kv_spec(BLOCK, 1, 3),
                *[sorted_spec(b, kind) for b in range(blocks) for kind in range(2)],
            ],
            out_specs=q_spec,
        ),
        out_shape=jax.ShapeDtypeStruct(queries.shape, jnp.bfloat16),
        compiler_params=pltpu.CompilerParams(vmem_limit_bytes=32 * 1024 * 1024),
    )(place, where, queries, own, own, prev, prev, *([arrived] * (2 * blocks)))


def local_gathered(tokens, queries, key_weight, value_weight, sorted_blocks):
    local_blocks = tokens.shape[1] // BLOCK
    devices = lax.axis_size("seq")
    me = lax.axis_index("seq")
    capacity = (KVH * local_blocks + devices - 1) // devices
    targets = sorted_blocks[0]
    wanted = plan_sends(lax.all_gather(targets, "seq", axis=0), me, local_blocks, capacity)
    place = plan_receives(targets, local_blocks, capacity)
    weights = lax.all_gather(
        jnp.concatenate([key_weight, value_weight], axis=1), ("fsdp", "seq"), axis=0, tiled=True
    )
    packed = jnp.dot(tokens[0], weights, preferred_element_type=jnp.float32).astype(jnp.bfloat16)
    own = jnp.stack([packed[:, : KVH * DH], packed[:, KVH * DH :]])[:, None]
    prev = lax.ppermute(own[:, :, -BLOCK:], "seq", [(i, i + 1) for i in range(devices - 1)])
    table = own.reshape(2, local_blocks, BLOCK, KVH, DH).transpose(3, 1, 0, 2, 4)
    replies = jnp.take(table.reshape(-1, 2, BLOCK, DH), wanted.reshape(-1), axis=0)
    arrived = lax.all_to_all(replies, "seq", split_axis=0, concat_axis=0, tiled=True)
    zero = jnp.zeros_like(me)
    where = jnp.stack([(me == 0).astype(jnp.int32), zero, zero, zero])
    return attend(place, where, queries[0], own, prev, arrived.transpose(1, 0, 2, 3))[None]


def project_kernel(pieces, column_ref, *refs):
    token_refs, refs = refs[:4], refs[4:]
    piece_refs, (keep_ref, send_ref, weights, total, sems) = refs[:pieces], refs[pieces:]
    step = pl.program_id(0)

    @pl.when(step == 0)
    def _():
        for i in range(pieces):
            pltpu.make_async_copy(piece_refs[i], weights.at[i], sems.at[i]).start()

    pltpu.make_async_copy(piece_refs[0], weights.at[step], sems.at[step]).wait()
    rows = token_refs[0].shape[0]
    for i, ref in enumerate(token_refs):
        product = jnp.dot(ref[...], weights[step], preferred_element_type=jnp.float32)

        @pl.when(step == 0)
        def _():
            total[i] = product

        @pl.when((step > 0) & (step < pieces - 1))
        def _():
            total[i] += product

        @pl.when(step == pieces - 1)
        def _():
            out_ref = keep_ref if i % 2 == 0 else send_ref
            out_ref[i // 2] = (total[i] + product).astype(jnp.bfloat16)


def project(columns, token_sets, pieces):
    tokens, depth, width = token_sets[0].shape[0], *pieces[0].shape
    spec = pl.BlockSpec((tokens, depth), lambda i, columns: (0, columns[i]))
    shape = (2, tokens, width)
    return pl.pallas_call(
        functools.partial(project_kernel, len(pieces)),
        grid_spec=pltpu.PrefetchScalarGridSpec(
            num_scalar_prefetch=1,
            grid=(len(pieces),),
            in_specs=[spec] * 4 + [pl.BlockSpec(memory_space=pl.ANY)] * len(pieces),
            out_specs=[pl.BlockSpec(shape, lambda i, columns: (0, 0, 0))] * 2,
            scratch_shapes=[
                pltpu.VMEM((len(pieces), depth, width), jnp.bfloat16),
                pltpu.VMEM((4, tokens, width), jnp.float32),
                pltpu.SemaphoreType.DMA((len(pieces),)),
            ],
        ),
        out_shape=[jax.ShapeDtypeStruct(shape, jnp.bfloat16)] * 2,
        compiler_params=pltpu.CompilerParams(vmem_limit_bytes=40 * 1024 * 1024),
    )(columns, *token_sets, *pieces)


def pack_kernel(items, row_ref, part_ref, mine_ref, other_ref, out_ref, sems):
    heads = mine_ref.shape[2] // DH
    blocks = mine_ref.shape[1] // BLOCK

    def copy(i, source_ref):
        row = row_ref[i]
        head, block = row // blocks, row % blocks
        source = source_ref.at[
            part_ref[0] ^ (i // (items // 2)),
            pl.ds(pl.multiple_of(block * BLOCK, BLOCK), BLOCK),
            pl.ds(pl.multiple_of((head % heads) * DH, DH), DH),
        ]
        return pltpu.make_async_copy(source, out_ref.at[i], sems.at[i])

    for i in range(items):
        part = (row_ref[i] // blocks // heads) ^ part_ref[1]

        @pl.when(part == 0)
        def _():
            copy(i, mine_ref).start()

        @pl.when(part != 0)
        def _():
            copy(i, other_ref).start()

    for i in range(items):
        copy(i, mine_ref).wait()


def pack(rows, part, mine, other):
    items = rows.shape[0]
    return pl.pallas_call(
        functools.partial(pack_kernel, items),
        grid_spec=pltpu.PrefetchScalarGridSpec(
            num_scalar_prefetch=2,
            grid=(),
            in_specs=[pl.BlockSpec(memory_space=pl.ANY)] * 2,
            out_specs=pl.BlockSpec(memory_space=pl.ANY),
            scratch_shapes=[pltpu.SemaphoreType.DMA((items,))],
        ),
        out_shape=jax.ShapeDtypeStruct((items, BLOCK, DH), jnp.bfloat16),
    )(rows, part, mine, other)


def local_split(tokens, queries, key_weight, value_weight, sorted_blocks):
    y, x, z, c = [lax.axis_index(name) for name in ("y", "x", "z", "c")]
    chips = lax.axis_size("z")
    devices = 2 * chips
    me = 2 * z + c
    local_tokens = tokens.shape[1]
    local_blocks = local_tokens // BLOCK
    capacity = (KVH * local_blocks + devices - 1) // devices
    half = KVH * DH // 2
    targets = sorted_blocks[0]
    swap = [(0, 1), (1, 0)]

    quarters = jnp.stack(
        [key_weight[:, :half], key_weight[:, half:], value_weight[:, :half], value_weight[:, half:]]
    )
    shared = lax.all_to_all(quarters, ("x", "c"), split_axis=0, concat_axis=0, tiled=True)
    x_tokens = lax.ppermute(tokens[0], "x", swap)
    c_tokens = lax.ppermute(tokens[0], "c", swap)
    xc_tokens = lax.ppermute(x_tokens, "c", swap)

    ring = [(i, (i + 1) % chips) for i in range(chips)]
    pieces, columns = [], []
    depth = 2 * key_weight.shape[0]
    held = [shared[2 * i : 2 * i + 2].reshape(depth, half) for i in range(2)]
    for step in range(chips):
        if step > 0:
            held = [lax.ppermute(value, "z", ring) for value in held]
        from_z = (z - step) % chips
        for i in range(2):
            pieces += [held[i], lax.ppermute(held[i], "y", swap)]
            columns += [(y * 2 + i) * chips + from_z, ((1 - y) * 2 + i) * chips + from_z]

    all_targets = lax.all_gather(targets, ("x", "z", "c"), axis=0).reshape(2, devices, KVH, local_blocks)
    wanted = [plan_sends(all_targets[i], me, local_blocks, capacity).reshape(-1) for i in range(2)]
    place = plan_receives(targets, local_blocks, capacity)

    mine, sent = project(
        jnp.stack(columns).astype(jnp.int32), [tokens[0], c_tokens, x_tokens, xc_tokens], pieces
    )
    other = lax.ppermute(sent, "c", swap)
    replies = pack(jnp.concatenate(wanted), jnp.stack([x, c]).astype(jnp.int32), mine, other)
    arrived = lax.all_to_all(replies, ("x", "z", "c"), split_axis=0, concat_axis=0, tiled=True)
    arrived = arrived.reshape(2, devices * capacity, BLOCK, DH)

    own = jnp.stack([mine[0], other[0]])
    own = jnp.stack([own, lax.ppermute(jnp.stack([mine[1], other[1]]), "x", swap)])
    prev = lax.ppermute(own[:, :, -BLOCK:], ("z", "c"), [(i, i + 1) for i in range(devices - 1)])
    where = jnp.stack([(me == 0).astype(jnp.int32), x, c, 1 - c]).astype(jnp.int32)
    return attend(place, where, queries[0], own, prev, arrived)[None]


def solution(mesh):
    fsdp, seq = mesh.shape["fsdp"], mesh.shape["seq"]
    if fsdp == 4 and seq % 2 == 0 and seq <= 8:
        mesh = Mesh(mesh.devices.reshape(2, 2, seq // 2, 2), ("y", "x", "z", "c"))
        step, fsdp, seq = local_split, ("y", "x"), ("z", "c")
    else:
        step, fsdp, seq = local_gathered, ("fsdp",), ("seq",)
    placed = (
        P(fsdp, seq, None),
        P(fsdp, seq, None),
        P((*fsdp, *seq), None),
        P((*fsdp, *seq), None),
        P(fsdp, None, seq),
    )
    return jax.shard_map(step, mesh=mesh, in_specs=placed, out_specs=P(fsdp, seq, None), check_vma=False)
```

```python
import functools
import math

import jax
import jax.numpy as jnp
from jax import lax
from jax.experimental import pallas as pl
from jax.experimental.pallas import tpu as pltpu
from jax.sharding import Mesh, PartitionSpec as P

DH = 128
KVH = 8
GROUP = 4
BLOCK = 128
TALL = 2 * BLOCK
EXP2_SCALE = math.log2(math.e) / math.sqrt(DH)


def plan_sends(all_targets, me, local_blocks, capacity):
    devices = all_targets.shape[0]
    targets = all_targets.reshape(devices, -1)
    heads = jnp.arange(targets.shape[1], dtype=jnp.int32) // local_blocks
    mine = targets // local_blocks == me
    rank = jnp.cumsum(mine.astype(jnp.int32), axis=1) - 1
    row = heads[None, :] * local_blocks + targets % local_blocks
    hit = mine[:, :, None] & (rank[:, :, None] == jnp.arange(capacity, dtype=jnp.int32))
    return jnp.sum(jnp.where(hit, row[:, :, None], 0), axis=1)


def plan_receives(targets, local_blocks, capacity):
    owner = targets.reshape(-1) // local_blocks
    order = jnp.arange(owner.shape[0], dtype=jnp.int32)
    same = (owner[:, None] == owner[None, :]) & (order[None, :] < order[:, None])
    return owner * capacity + jnp.sum(same.astype(jnp.int32), axis=1)


def group_rows(head, b, part):
    for i in range(TALL // BLOCK):
        group = head * GROUP + part * (TALL // BLOCK) + i
        yield i, (pl.ds(b * BLOCK, BLOCK), pl.ds(group * DH, DH))


def ahead(runs, score, finish):
    scores = score(*runs[0])
    for now, later in zip(runs, runs[1:] + [None], strict=True):
        held, scores = scores, score(*later) if later else None
        finish(*now, held)


def near_kernel(where_ref, q_ref, k_ref, v_ref, pk_ref, pv_ref, out_ref, log_ref):
    blocks = k_ref.shape[2] // BLOCK
    heads = k_ref.shape[3] // DH
    lane = lax.broadcasted_iota(jnp.int32, (BLOCK, DH), 1)
    logs = [jnp.zeros((BLOCK, DH), jnp.float32) for _ in range(blocks)]

    def load(ref, prev_ref, head, b):
        own, before = pl.ds(b * BLOCK, BLOCK), pl.ds((b - 1) * BLOCK, BLOCK)
        columns = pl.ds(head * DH, DH)
        prev = prev_ref[0, 0, :, columns] if b == 0 else ref[0, 0, before, columns]
        return jnp.concatenate([ref[0, 0, own, columns], prev], axis=0)

    def score(head, b, part):
        q = jnp.concatenate([q_ref[at] for _, at in group_rows(head, b, part)], axis=0)
        keys = load(k_ref, pk_ref, head, b)
        scores = lax.dot_general(q, keys, (((1,), (1,)), ((), ())), preferred_element_type=jnp.float32)
        if b == 0:
            column = lax.broadcasted_iota(jnp.int32, (1, 2 * BLOCK), 1)
            scores = jnp.where((column >= BLOCK) & (where_ref[0] == 1), -1e30, scores)
        return scores

    def finish(head, b, part, scores):
        highest = jnp.max(scores, axis=-1, keepdims=True)
        raised = jnp.exp2((scores - highest) * EXP2_SCALE)
        total = jnp.sum(raised, axis=-1, keepdims=True)
        log = highest * EXP2_SCALE + jnp.log2(total)
        values = load(v_ref, pv_ref, head, b)
        result = jnp.dot(raised.astype(jnp.bfloat16), values, preferred_element_type=jnp.float32) * (1.0 / total)
        for i, at in group_rows(head, b, part):
            rows = slice(i * BLOCK, (i + 1) * BLOCK)
            out_ref[at] = result[rows]
            logs[b] = jnp.where(lane == head * GROUP + part * (TALL // BLOCK) + i, log[rows], logs[b])

    ahead([(h, b, p) for h in range(heads) for b in range(blocks) for p in range(GROUP * BLOCK // TALL)], score, finish)
    for b in range(blocks):
        log_ref[pl.ds(b * BLOCK, BLOCK)] = logs[b]


def far_kernel(place_ref, where_ref, q_ref, near_ref, log_ref, *rest):
    sorted_refs, out_ref = rest[:-1], rest[-1]
    blocks = q_ref.shape[0] // BLOCK
    heads = q_ref.shape[1] // (GROUP * DH)
    lane = lax.broadcasted_iota(jnp.int32, (BLOCK, DH), 1)

    def load(head, b, kind):
        return sorted_refs[2 * (head * blocks + b) + kind][0, 0]

    def score(head, b, part):
        q = jnp.concatenate([q_ref[at] for _, at in group_rows(head, b, part)], axis=0)
        return lax.dot_general(
            q, load(head, b, 0), (((1,), (1,)), ((), ())), preferred_element_type=jnp.float32
        )

    def finish(head, b, part, scores):
        spots = list(group_rows(head, b, part))
        picks = [
            jnp.where(lane == head * GROUP + part * (TALL // BLOCK) + i, log_ref[at[0]], 0.0) for i, at in spots
        ]
        log = jnp.sum(jnp.concatenate(picks, axis=0), axis=-1, keepdims=True)
        near = jnp.concatenate([near_ref[at] for _, at in spots], axis=0)
        highest = jnp.maximum(jnp.max(scores, axis=-1, keepdims=True) * EXP2_SCALE, log)
        raised = jnp.exp2(scores * EXP2_SCALE - highest)
        share = jnp.exp2(log - highest)
        scale = 1.0 / (share + jnp.sum(raised, axis=-1, keepdims=True))
        far = jnp.dot(raised.astype(jnp.bfloat16), load(head, b, 1), preferred_element_type=jnp.float32)
        result = (near * (share * scale) + far * scale).astype(jnp.bfloat16)
        for i, at in spots:
            out_ref[at] = result[i * BLOCK : (i + 1) * BLOCK]

    ahead([(h, b, p) for h in range(heads) for b in range(blocks) for p in range(GROUP * BLOCK // TALL)], score, finish)


def attend(place, where, queries, own, prev, arrived):
    tokens, columns = queries.shape
    blocks = tokens // BLOCK
    step = 2
    width = step * GROUP * DH
    steps = own.shape[3] // (step * DH)

    def kv_spec(rows, kind, at):
        def index(h, where):
            return (where[1] ^ kind, (h // steps) ^ where[at], 0, h % steps)

        return pl.BlockSpec((1, 1, rows, step * DH), index)

    def sorted_spec(item, kind):
        return pl.BlockSpec(
            (1, 1, BLOCK, DH), lambda h, place, where: (place[h * step * blocks + item], kind, 0, 0)
        )

    near, logs = pl.pallas_call(
        near_kernel,
        grid_spec=pltpu.PrefetchScalarGridSpec(
            num_scalar_prefetch=1,
            grid=(KVH // step,),
            in_specs=[
                pl.BlockSpec((tokens, width), lambda h, where: (0, h)),
                kv_spec(tokens, 0, 2),
                kv_spec(tokens, 1, 2),
                kv_spec(BLOCK, 0, 3),
                kv_spec(BLOCK, 1, 3),
            ],
            out_specs=[
                pl.BlockSpec((tokens, width), lambda h, where: (0, h)),
                pl.BlockSpec((tokens, DH), lambda h, where: (0, h)),
            ],
        ),
        out_shape=[
            jax.ShapeDtypeStruct(queries.shape, jnp.float32),
            jax.ShapeDtypeStruct((tokens, KVH // step * DH), jnp.float32),
        ],
        cost_estimate=pl.CostEstimate(
            flops=8 * tokens * columns * BLOCK, bytes_accessed=8 * tokens * columns, transcendentals=2 * tokens * columns
        ),
        compiler_params=pltpu.CompilerParams(vmem_limit_bytes=24 * 1024 * 1024),
    )(where, queries, own, own, prev, prev)
    q_spec = pl.BlockSpec((tokens, width), lambda h, place, where: (0, h))
    return pl.pallas_call(
        far_kernel,
        grid_spec=pltpu.PrefetchScalarGridSpec(
            num_scalar_prefetch=2,
            grid=(KVH // step,),
            in_specs=[
                q_spec,
                q_spec,
                pl.BlockSpec((tokens, DH), lambda h, place, where: (0, h)),
                *[sorted_spec(item, kind) for item in range(step * blocks) for kind in range(2)],
            ],
            out_specs=q_spec,
        ),
        out_shape=jax.ShapeDtypeStruct(queries.shape, jnp.bfloat16),
        cost_estimate=pl.CostEstimate(
            flops=4 * tokens * columns * BLOCK, bytes_accessed=8 * tokens * columns, transcendentals=tokens * columns
        ),
        compiler_params=pltpu.CompilerParams(vmem_limit_bytes=24 * 1024 * 1024),
    )(place, where, queries, near, logs, *([arrived] * (2 * step * blocks)))


def local_gathered(tokens, queries, key_weight, value_weight, sorted_blocks):
    local_blocks = tokens.shape[1] // BLOCK
    devices = lax.axis_size("seq")
    me = lax.axis_index("seq")
    capacity = (KVH * local_blocks + devices - 1) // devices
    targets = sorted_blocks[0]
    wanted = plan_sends(lax.all_gather(targets, "seq", axis=0), me, local_blocks, capacity)
    place = plan_receives(targets, local_blocks, capacity)
    weights = lax.all_gather(
        jnp.concatenate([key_weight, value_weight], axis=1), ("fsdp", "seq"), axis=0, tiled=True
    )
    packed = jnp.dot(tokens[0], weights, preferred_element_type=jnp.float32).astype(jnp.bfloat16)
    own = jnp.stack([packed[:, : KVH * DH], packed[:, KVH * DH :]])[:, None]
    prev = lax.ppermute(own[:, :, -BLOCK:], "seq", [(i, i + 1) for i in range(devices - 1)])
    table = own.reshape(2, local_blocks, BLOCK, KVH, DH).transpose(3, 1, 0, 2, 4)
    replies = jnp.take(table.reshape(-1, 2, BLOCK, DH), wanted.reshape(-1), axis=0)
    arrived = lax.all_to_all(replies, "seq", split_axis=0, concat_axis=0, tiled=True)
    zero = jnp.zeros_like(me)
    where = jnp.stack([(me == 0).astype(jnp.int32), zero, zero, zero])
    return attend(place, where, queries[0], own, prev, arrived)[None]


def project_kernel(runs, arrays, pieces, place_ref, *refs):
    token_refs, array_refs = refs[:runs], refs[runs : runs + arrays]
    out_refs, (tokens, weights, token_sems, piece_sems) = refs[runs + arrays : -4], refs[-4:]
    depth = weights.shape[0] // len(pieces)
    tall = out_refs[0].shape[0] // 2
    arrivals, copies, start = [], [], 0
    for i, (array, first) in enumerate(pieces):
        rows = pl.ds(pl.multiple_of(place_ref[i] * depth, depth), depth)
        source = array_refs[array].at[pl.ds(first, depth)]
        arrivals.append(pltpu.make_async_copy(source, weights.at[rows], piece_sems.at[i]))
    for i, ref in enumerate(token_refs):
        rows = ref.shape[0]
        copy = pltpu.make_async_copy(ref, tokens.at[pl.ds(start, rows)], token_sems.at[i])
        copies.append((copy, start // tall))
        start += rows
    for copy in arrivals:
        copy.start()
    for copy, _ in copies:
        copy.start()
    for copy in arrivals:
        copy.wait()
    for i in range(2 * len(out_refs)):
        for copy, of in copies:
            if of == i:
                copy.wait()
        product = jnp.dot(tokens[i * tall : (i + 1) * tall], weights[...], preferred_element_type=jnp.float32)
        out_refs[i // 2][i % 2 * tall : (i % 2 + 1) * tall] = product.astype(jnp.bfloat16)


def project(token_runs, arrays, pieces, places):
    tokens = sum(run.shape[0] for run in token_runs)
    depth, width = token_runs[0].shape[1], arrays[0].shape[1]
    anywhere = pl.BlockSpec(memory_space=pl.ANY)
    return pl.pallas_call(
        functools.partial(project_kernel, len(token_runs), len(arrays), pieces),
        grid_spec=pltpu.PrefetchScalarGridSpec(
            num_scalar_prefetch=1,
            grid=(),
            in_specs=[anywhere] * (len(token_runs) + len(arrays)),
            out_specs=[pl.BlockSpec(memory_space=pltpu.VMEM)] * 2,
            scratch_shapes=[
                pltpu.VMEM((tokens, depth), jnp.bfloat16),
                pltpu.VMEM((depth, width), jnp.bfloat16),
                pltpu.SemaphoreType.DMA((len(token_runs),)),
                pltpu.SemaphoreType.DMA((len(pieces),)),
            ],
        ),
        out_shape=[jax.ShapeDtypeStruct((tokens // 2, width), jnp.bfloat16)] * 2,
        cost_estimate=pl.CostEstimate(
            flops=2 * tokens * depth * width, bytes_accessed=2 * (tokens + width) * depth, transcendentals=0
        ),
        compiler_params=pltpu.CompilerParams(vmem_limit_bytes=60 * 1024 * 1024),
    )(places, *token_runs, *arrays)


def pack_kernel(row_ref, part_ref, *refs):
    half_refs, out_ref, table = refs[:4], refs[4], refs[5]
    heads = table.shape[3] // DH
    blocks = table.shape[2] // BLOCK
    for i, ref in enumerate(half_refs):
        table[i // 2, i % 2] = ref[...]
    for i in range(row_ref.shape[0]):
        head, block = row_ref[i] // blocks, row_ref[i] % blocks
        for kind in range(2):
            out_ref[i, kind] = table[
                part_ref[0] ^ kind,
                (head // heads) ^ part_ref[1],
                pl.ds(pl.multiple_of(block * BLOCK, BLOCK), BLOCK),
                pl.ds(pl.multiple_of((head % heads) * DH, DH), DH),
            ]


def pack(rows, part, halves):
    return pl.pallas_call(
        pack_kernel,
        grid_spec=pltpu.PrefetchScalarGridSpec(
            num_scalar_prefetch=2,
            grid=(),
            in_specs=[pl.BlockSpec(memory_space=pltpu.VMEM)] * 4,
            out_specs=pl.BlockSpec(memory_space=pltpu.VMEM),
            scratch_shapes=[pltpu.VMEM((2, 2, *halves[0].shape), jnp.bfloat16)],
        ),
        out_shape=jax.ShapeDtypeStruct((rows.shape[0], 2, BLOCK, DH), jnp.bfloat16),
        compiler_params=pltpu.CompilerParams(vmem_limit_bytes=16 * 1024 * 1024),
    )(rows, part, *halves)


def local_split(tokens, queries, key_weight, value_weight, sorted_blocks):
    y, x, z, c = [lax.axis_index(name) for name in ("y", "x", "z", "c")]
    chips = lax.axis_size("z")
    devices = 2 * chips
    me = 2 * z + c
    local_blocks = tokens.shape[1] // BLOCK
    capacity = (KVH * local_blocks + devices - 1) // devices
    half = KVH * DH // 2
    targets = sorted_blocks[0]

    near = jnp.where(x == 0, key_weight, value_weight)
    away = jnp.where(x == 0, value_weight, key_weight)

    def part(weight, core):
        return lax.dynamic_slice_in_dim(weight, core * half, half, 1)

    def along(axis, step):
        count = lax.axis_size(axis)
        return lambda value: lax.ppermute(value, axis, [(i, (i + step) % count) for i in range(count)])

    over_x, over_y, over_c, up, down = along("x", 1), along("y", 1), along("c", 1), along("z", 1), along("z", -1)

    def over_xc(value):
        return lax.ppermute(value, ("x", "c"), [(i, 3 - i) for i in range(4)])

    def by_core(same_core, other_core):
        pair = jnp.stack([same_core, other_core])
        return jnp.where(c == 0, pair, pair[::-1])

    rows = key_weight.shape[0]
    notes = jnp.zeros((16, half), jnp.bfloat16).at[0, : targets.size].set(targets.reshape(-1).astype(jnp.bfloat16))
    from_x, from_xc = over_x(part(away, c)), over_xc(part(away, 1 - c))
    from_c = over_c(jnp.concatenate([part(near, 1 - c), notes]))
    ours = by_core(part(near, c), from_c[:rows]).reshape(-1, half)
    theirs = by_core(from_x, from_xc).reshape(-1, half)
    notes = by_core(notes[:1], from_c[rows : rows + 1]).reshape(-1, half)
    unit = jnp.concatenate([ours, theirs, notes, jnp.zeros((14, half), jnp.bfloat16)])

    early, late = jnp.split(tokens[0], 2)
    early, late, unit = lax.optimization_barrier((early, late, unit))
    x_early = over_x(early)
    x_late = over_x(late)
    c_tokens = over_c(tokens[0])

    deep = 2 * rows
    from_up, from_down = up(unit), down(unit)
    y_unit = over_y(unit)
    from_up, y_unit = lax.optimization_barrier((from_up, y_unit))
    y_up = over_y(from_up)
    from_down, y_up, x_early = lax.optimization_barrier((from_down, y_up, x_early))
    y_down = over_y(from_down)
    far_ours, far_theirs = up(from_up[:deep]), down(from_down[deep:])
    far_ours, y_down = lax.optimization_barrier((far_ours, y_down))
    y_ours, y_theirs = over_y(far_ours), over_y(far_theirs)
    x_late, far_theirs, y_ours, y_theirs = lax.optimization_barrier((x_late, far_theirs, y_ours, y_theirs))
    arrays, pieces, places = [], [], []
    for value, across, from_z, kinds in (
        (unit, y_unit, z, (0, 1)),
        (from_up, y_up, z - 1, (0, 1)),
        (from_down, y_down, z + 1, (0, 1)),
        (far_ours, y_ours, z + 2, (0,)),
        (far_theirs, y_theirs, z + 2, (1,)),
    ):
        for array, from_y in ((value, y), (across, 1 - y)):
            for i, kind in enumerate(kinds):
                pieces.append((len(arrays), i * deep))
                places.append((from_y * 2 + (x ^ kind)) * chips + from_z % chips)
            arrays.append(array)
    places = jnp.stack(places).astype(jnp.int32)
    xc_early = over_c(x_early)
    xc_late = over_c(x_late)

    notes = jnp.stack([unit[2 * deep :], from_up[2 * deep :], from_down[2 * deep :], far_theirs[deep:]])
    notes = notes[:, :2, : targets.size].astype(jnp.int32)
    from_z = (z + jnp.array([0, -1, 1, 2], jnp.int32)) % chips
    own_row = from_z[:, None] == jnp.arange(chips, dtype=jnp.int32)[None]
    all_targets = jnp.sum(jnp.where(own_row[:, :, None, None], notes[:, None], 0), axis=0)
    wanted = plan_sends(all_targets.reshape(devices, *targets.shape), me, local_blocks, capacity).reshape(-1)
    place = plan_receives(targets, local_blocks, capacity)

    x_sent, xc_sent = project([x_early, x_late, xc_early, xc_late], arrays, pieces, places)
    x_same, x_diff = over_x(x_sent), over_xc(xc_sent)
    own_tokens, x_sent = lax.optimization_barrier((tokens[0], x_sent))
    same, sent = project([own_tokens, c_tokens], arrays, pieces, places)
    halves = [same, over_c(sent), x_same, x_diff]
    replies = pack(wanted, jnp.stack([x, c]).astype(jnp.int32), halves)
    arrived = lax.all_to_all(replies, ("z", "c"), split_axis=0, concat_axis=0, tiled=True)

    own = jnp.stack(halves).reshape(2, 2, *same.shape)
    prev = lax.ppermute(own[:, :, -BLOCK:], ("z", "c"), [(i, i + 1) for i in range(devices - 1)])
    where = jnp.stack([(me == 0).astype(jnp.int32), x, c, 1 - c]).astype(jnp.int32)
    return attend(place, where, queries[0], own, prev, arrived)[None]


def solution(mesh):
    fsdp, seq = mesh.shape["fsdp"], mesh.shape["seq"]
    if (fsdp, seq) == (4, 8):
        mesh = Mesh(mesh.devices.reshape(2, 2, seq // 2, 2), ("y", "x", "z", "c"))
        step, fsdp, seq = local_split, ("y", "x"), ("z", "c")
    else:
        step, fsdp, seq = local_gathered, ("fsdp",), ("seq",)
    placed = (
        P(fsdp, seq, None),
        P(fsdp, seq, None),
        P((*fsdp, *seq), None),
        P((*fsdp, *seq), None),
        P(fsdp, None, seq),
    )
    return jax.shard_map(step, mesh=mesh, in_specs=placed, out_specs=P(fsdp, seq, None), check_vma=False)
```

```python
import functools
import math

import jax
import jax.numpy as jnp
from jax import lax
from jax.experimental import pallas as pl
from jax.experimental.pallas import tpu as pltpu
from jax.sharding import Mesh, PartitionSpec as P

DH = 128
KVH = 8
GROUP = 4
BLOCK = 128
TALL = GROUP * BLOCK
DIGITS = 3
EXP2_SCALE = math.log2(math.e) / math.sqrt(DH)


def plan_sends(all_targets, me, local_blocks, capacity):
    devices = all_targets.shape[0]
    targets = all_targets.reshape(devices, -1)
    heads = jnp.arange(targets.shape[1], dtype=jnp.int32) // local_blocks
    mine = targets // local_blocks == me
    rank = jnp.cumsum(mine.astype(jnp.int32), axis=1) - 1
    row = heads[None, :] * local_blocks + targets % local_blocks
    hit = mine[:, :, None] & (rank[:, :, None] == jnp.arange(capacity, dtype=jnp.int32))
    return jnp.sum(jnp.where(hit, row[:, :, None], 0), axis=1)


def plan_receives(targets, local_blocks, capacity):
    owner = targets.reshape(-1) // local_blocks
    order = jnp.arange(owner.shape[0], dtype=jnp.int32)
    same = (owner[:, None] == owner[None, :]) & (order[None, :] < order[:, None])
    return owner * capacity + jnp.sum(same.astype(jnp.int32), axis=1)


def group_rows(head, b, part):
    for i in range(TALL // BLOCK):
        group = head * GROUP + part * (TALL // BLOCK) + i
        yield i, (pl.ds(b * BLOCK, BLOCK), pl.ds(group * DH, DH))


def ahead(runs, score, finish):
    scores = score(*runs[0])
    for now, later in zip(runs, runs[1:] + [None], strict=True):
        held, scores = scores, score(*later) if later else None
        finish(*now, held)


def weighted(raised, values):
    both = jnp.concatenate([values, jnp.ones_like(values)], axis=1)
    result = jnp.dot(raised.astype(jnp.bfloat16), both, preferred_element_type=jnp.float32)
    return result[:, :DH], result[:, DH:]


def near_kernel(where_ref, q_ref, k_ref, v_ref, pk_ref, pv_ref, out_ref, log_ref):
    blocks = k_ref.shape[2] // BLOCK
    heads = k_ref.shape[3] // DH
    lane = lax.broadcasted_iota(jnp.int32, (BLOCK, DH), 1)
    logs = [jnp.zeros((BLOCK, DH), jnp.float32) for _ in range(blocks)]

    def load(ref, prev_ref, head, b):
        own, before = pl.ds(b * BLOCK, BLOCK), pl.ds((b - 1) * BLOCK, BLOCK)
        columns = pl.ds(head * DH, DH)
        prev = prev_ref[0, 0, :, columns] if b == 0 else ref[0, 0, before, columns]
        return jnp.concatenate([ref[0, 0, own, columns], prev], axis=0)

    def score(head, b, part):
        q = jnp.concatenate([q_ref[at] for _, at in group_rows(head, b, part)], axis=0)
        keys = load(k_ref, pk_ref, head, b)
        scores = lax.dot_general(q, keys, (((1,), (1,)), ((), ())), preferred_element_type=jnp.float32)
        if b == 0:
            column = lax.broadcasted_iota(jnp.int32, (1, 2 * BLOCK), 1)
            scores = jnp.where((column >= BLOCK) & (where_ref[0] == 1), -1e30, scores)
        return scores

    def finish(head, b, part, scores):
        highest = jnp.max(scores, axis=-1, keepdims=True)
        raised = jnp.exp2((scores - highest) * EXP2_SCALE)
        result, total = weighted(raised, load(v_ref, pv_ref, head, b))
        result = result * (1.0 / total)
        log = highest * EXP2_SCALE + jnp.log2(total)
        for i, at in group_rows(head, b, part):
            rows = slice(i * BLOCK, (i + 1) * BLOCK)
            out_ref[at] = result[rows]
            group, rest = head * GROUP + part * (TALL // BLOCK) + i, log[rows]
            for digit in range(DIGITS):
                rounded = rest.astype(jnp.bfloat16).astype(jnp.float32)
                logs[b] = jnp.where(lane == digit * heads * GROUP + group, rounded, logs[b])
                rest = rest - rounded

    ahead([(h, b, p) for h in range(heads) for b in range(blocks) for p in range(GROUP * BLOCK // TALL)], score, finish)
    for b in range(blocks):
        log_ref[pl.ds(b * BLOCK, BLOCK)] = logs[b].astype(jnp.bfloat16)


def far_kernel(arrays, place_ref, where_ref, q_ref, near_ref, log_ref, spread_ref, *refs):
    array_refs, (out_ref, table) = refs[:arrays], refs[arrays:]
    blocks = q_ref.shape[0] // BLOCK
    heads = q_ref.shape[1] // (GROUP * DH)
    first = pl.program_id(0) * heads * blocks

    @pl.when(pl.program_id(0) == 0)
    def _():
        for i, ref in enumerate(array_refs):
            kind, start = i // (arrays // 2), i % (arrays // 2) * ref.shape[0]
            table[kind, pl.ds(start, ref.shape[0])] = ref[...]

    logs = [
        jnp.dot(log_ref[pl.ds(b * BLOCK, BLOCK)], spread_ref[...], preferred_element_type=jnp.float32)
        for b in range(blocks)
    ]

    def load(head, b, kind):
        return table[where_ref[1] ^ kind, place_ref[first + head * blocks + b]]

    def score(head, b, part):
        q = jnp.concatenate([q_ref[at] for _, at in group_rows(head, b, part)], axis=0)
        return lax.dot_general(
            q, load(head, b, 0), (((1,), (1,)), ((), ())), preferred_element_type=jnp.float32
        )

    def finish(head, b, part, scores):
        spots = list(group_rows(head, b, part))
        log = jnp.concatenate([logs[b][:, at[1].start : at[1].start + DH] for _, at in spots], axis=0)
        near = jnp.concatenate([near_ref[at] for _, at in spots], axis=0)
        highest = jnp.maximum(jnp.max(scores, axis=-1, keepdims=True) * EXP2_SCALE, log)
        far, total = weighted(jnp.exp2(scores * EXP2_SCALE - highest), load(head, b, 1))
        share = jnp.exp2(log - highest)
        result = ((near * share + far) * (1.0 / (share + total))).astype(jnp.bfloat16)
        for i, at in spots:
            out_ref[at] = result[i * BLOCK : (i + 1) * BLOCK]

    ahead([(h, b, p) for h in range(heads) for b in range(blocks) for p in range(GROUP * BLOCK // TALL)], score, finish)


def attend(place, where, queries, own, prev, arrived):
    tokens, columns = queries.shape
    blocks = tokens // BLOCK
    step = 4
    width = step * GROUP * DH
    steps = own.shape[3] // (step * DH)

    def kv_spec(rows, kind, at):
        def index(h, where):
            return (where[1] ^ kind, (h // steps) ^ where[at], 0, h % steps)

        return pl.BlockSpec((1, 1, rows, step * DH), index)

    near, logs = pl.pallas_call(
        near_kernel,
        grid_spec=pltpu.PrefetchScalarGridSpec(
            num_scalar_prefetch=1,
            grid=(KVH // step,),
            in_specs=[
                pl.BlockSpec((tokens, width), lambda h, where: (0, h)),
                kv_spec(tokens, 0, 2),
                kv_spec(tokens, 1, 2),
                kv_spec(BLOCK, 0, 3),
                kv_spec(BLOCK, 1, 3),
            ],
            out_specs=[
                pl.BlockSpec((tokens, width), lambda h, where: (0, h)),
                pl.BlockSpec((tokens, DH), lambda h, where: (0, h)),
            ],
        ),
        out_shape=[
            jax.ShapeDtypeStruct(queries.shape, jnp.float32),
            jax.ShapeDtypeStruct((tokens, KVH // step * DH), jnp.bfloat16),
        ],
        cost_estimate=pl.CostEstimate(
            flops=8 * tokens * columns * BLOCK, bytes_accessed=8 * tokens * columns, transcendentals=2 * tokens * columns
        ),
        compiler_params=pltpu.CompilerParams(vmem_limit_bytes=24 * 1024 * 1024),
    )(where, queries, own, own, prev, prev)
    q_spec = pl.BlockSpec((tokens, width), lambda h, place, where: (0, h))
    digit = jnp.arange(DH)[:, None] - jnp.arange(width)[None] // DH
    groups = step * GROUP
    spread = ((digit >= 0) & (digit % groups == 0) & (digit < DIGITS * groups)).astype(jnp.bfloat16)
    return pl.pallas_call(
        functools.partial(far_kernel, len(arrived)),
        grid_spec=pltpu.PrefetchScalarGridSpec(
            num_scalar_prefetch=2,
            grid=(KVH // step,),
            in_specs=[
                q_spec,
                q_spec,
                pl.BlockSpec((tokens, DH), lambda h, place, where: (0, h)),
                pl.BlockSpec(spread.shape, lambda h, place, where: (0, 0)),
                *[pl.BlockSpec(array.shape, lambda h, place, where: (0, 0, 0)) for array in arrived],
            ],
            out_specs=q_spec,
            scratch_shapes=[
                pltpu.VMEM((2, sum(array.shape[0] for array in arrived) // 2, BLOCK, DH), jnp.bfloat16),
            ],
        ),
        out_shape=jax.ShapeDtypeStruct(queries.shape, jnp.bfloat16),
        cost_estimate=pl.CostEstimate(
            flops=4 * tokens * columns * BLOCK, bytes_accessed=8 * tokens * columns, transcendentals=tokens * columns
        ),
        compiler_params=pltpu.CompilerParams(vmem_limit_bytes=24 * 1024 * 1024),
    )(place, where, queries, near, logs, spread, *arrived)


def local_gathered(tokens, queries, key_weight, value_weight, sorted_blocks):
    local_blocks = tokens.shape[1] // BLOCK
    devices = lax.axis_size("seq")
    me = lax.axis_index("seq")
    capacity = (KVH * local_blocks + devices - 1) // devices
    targets = sorted_blocks[0]
    wanted = plan_sends(lax.all_gather(targets, "seq", axis=0), me, local_blocks, capacity)
    place = plan_receives(targets, local_blocks, capacity)
    weights = lax.all_gather(
        jnp.concatenate([key_weight, value_weight], axis=1), ("fsdp", "seq"), axis=0, tiled=True
    )
    packed = jnp.dot(tokens[0], weights, preferred_element_type=jnp.float32).astype(jnp.bfloat16)
    own = jnp.stack([packed[:, : KVH * DH], packed[:, KVH * DH :]])[:, None]
    prev = lax.ppermute(own[:, :, -BLOCK:], "seq", [(i, i + 1) for i in range(devices - 1)])
    table = own.reshape(2, local_blocks, BLOCK, KVH, DH).transpose(3, 1, 0, 2, 4)
    replies = jnp.take(table.reshape(-1, 2, BLOCK, DH), wanted.reshape(-1), axis=0)
    arrived = lax.all_to_all(replies, "seq", split_axis=0, concat_axis=0, tiled=True)
    zero = jnp.zeros_like(me)
    where = jnp.stack([(me == 0).astype(jnp.int32), zero, zero, zero])
    return attend(place, where, queries[0], own, prev, [arrived[:, 0], arrived[:, 1]])[None]


def project_kernel(runs, arrays, pieces, place_ref, *refs):
    token_refs, array_refs = refs[:runs], refs[runs : runs + arrays]
    out_refs, (tokens, weights, token_sems, piece_sems) = refs[runs + arrays : -4], refs[-4:]
    depth = weights.shape[0] // len(pieces)
    tall = out_refs[0].shape[0] // 2
    arrivals, copies, start = [], [], 0
    for i, (array, first) in enumerate(pieces):
        rows = pl.ds(pl.multiple_of(place_ref[i] * depth, depth), depth)
        source = array_refs[array].at[pl.ds(first, depth)]
        arrivals.append(pltpu.make_async_copy(source, weights.at[rows], piece_sems.at[i]))
    for i, ref in enumerate(token_refs):
        rows = ref.shape[0]
        copy = pltpu.make_async_copy(ref, tokens.at[pl.ds(start, rows)], token_sems.at[i])
        copies.append((copy, start // tall))
        start += rows
    for copy in arrivals:
        copy.start()
    for copy, _ in copies:
        copy.start()
    for copy in arrivals:
        copy.wait()
    for i in range(2 * len(out_refs)):
        for copy, of in copies:
            if of == i:
                copy.wait()
        product = jnp.dot(tokens[i * tall : (i + 1) * tall], weights[...], preferred_element_type=jnp.float32)
        out_refs[i // 2][i % 2 * tall : (i % 2 + 1) * tall] = product.astype(jnp.bfloat16)


def project(token_runs, arrays, pieces, places):
    tokens = sum(run.shape[0] for run in token_runs)
    depth, width = token_runs[0].shape[1], arrays[0].shape[1]
    anywhere = pl.BlockSpec(memory_space=pl.ANY)
    return pl.pallas_call(
        functools.partial(project_kernel, len(token_runs), len(arrays), pieces),
        grid_spec=pltpu.PrefetchScalarGridSpec(
            num_scalar_prefetch=1,
            grid=(),
            in_specs=[anywhere] * (len(token_runs) + len(arrays)),
            out_specs=[pl.BlockSpec(memory_space=pltpu.VMEM)] * 2,
            scratch_shapes=[
                pltpu.VMEM((tokens, depth), jnp.bfloat16),
                pltpu.VMEM((depth, width), jnp.bfloat16),
                pltpu.SemaphoreType.DMA((len(token_runs),)),
                pltpu.SemaphoreType.DMA((len(pieces),)),
            ],
        ),
        out_shape=[jax.ShapeDtypeStruct((tokens // 2, width), jnp.bfloat16)] * 2,
        cost_estimate=pl.CostEstimate(
            flops=2 * tokens * depth * width, bytes_accessed=2 * (tokens + width) * depth, transcendentals=0
        ),
        compiler_params=pltpu.CompilerParams(vmem_limit_bytes=60 * 1024 * 1024),
    )(places, *token_runs, *arrays)


def pack_kernel(row_ref, part_ref, same_ref, diff_ref, *refs):
    out_refs, table = refs[:-1], refs[-1]
    heads = table.shape[2] // DH
    blocks = table.shape[1] // BLOCK
    capacity = out_refs[0].shape[0]
    table[0] = same_ref[...]
    table[1] = diff_ref[...]
    for i in range(row_ref.shape[0]):
        head, block = row_ref[i] // blocks, row_ref[i] % blocks
        out_refs[i // capacity][i % capacity] = table[
            (head // heads) ^ part_ref[0],
            pl.ds(pl.multiple_of(block * BLOCK, BLOCK), BLOCK),
            pl.ds(pl.multiple_of((head % heads) * DH, DH), DH),
        ]


def pack(wanted, part, same, diff):
    devices, capacity = wanted.shape
    return pl.pallas_call(
        pack_kernel,
        grid_spec=pltpu.PrefetchScalarGridSpec(
            num_scalar_prefetch=2,
            grid=(),
            in_specs=[pl.BlockSpec(memory_space=pltpu.VMEM)] * 2,
            out_specs=[pl.BlockSpec(memory_space=pltpu.VMEM)] * devices,
            scratch_shapes=[pltpu.VMEM((2, *same.shape), jnp.bfloat16)],
        ),
        out_shape=[jax.ShapeDtypeStruct((capacity, BLOCK, DH), jnp.bfloat16)] * devices,
        compiler_params=pltpu.CompilerParams(vmem_limit_bytes=16 * 1024 * 1024),
    )(wanted.reshape(-1), part, same, diff)


def local_split(tokens, queries, key_weight, value_weight, sorted_blocks):
    y, x, z, c = [lax.axis_index(name) for name in ("y", "x", "z", "c")]
    chips = lax.axis_size("z")
    devices = 2 * chips
    me = 2 * z + c
    local_blocks = tokens.shape[1] // BLOCK
    capacity = (KVH * local_blocks + devices - 1) // devices
    half = KVH * DH // 2
    targets = sorted_blocks[0]

    near = jnp.where(x == 0, key_weight, value_weight)
    away = jnp.where(x == 0, value_weight, key_weight)

    def part(weight, core):
        return lax.dynamic_slice_in_dim(weight, core * half, half, 1)

    def along(axis, step):
        count = lax.axis_size(axis)
        return lambda value: lax.ppermute(value, axis, [(i, (i + step) % count) for i in range(count)])

    over_x, over_y, over_c, up, down = along("x", 1), along("y", 1), along("c", 1), along("z", 1), along("z", -1)

    def over_xc(value):
        return lax.ppermute(value, ("x", "c"), [(i, 3 - i) for i in range(4)])

    def by_core(same_core, other_core):
        pair = jnp.stack([same_core, other_core])
        return jnp.where(c == 0, pair, pair[::-1])

    rows = key_weight.shape[0]
    notes = jnp.zeros((16, half), jnp.bfloat16).at[0, : targets.size].set(targets.reshape(-1).astype(jnp.bfloat16))
    from_x, from_xc = over_x(part(away, c)), over_xc(part(away, 1 - c))
    from_c = over_c(jnp.concatenate([part(near, 1 - c), notes]))
    ours = by_core(part(near, c), from_c[:rows]).reshape(-1, half)
    theirs = by_core(from_x, from_xc).reshape(-1, half)
    notes = by_core(notes[:1], from_c[rows : rows + 1]).reshape(-1, half)
    unit = jnp.concatenate([ours, theirs, notes, jnp.zeros((14, half), jnp.bfloat16)])

    early, late = jnp.split(tokens[0], 2)
    early, late, unit = lax.optimization_barrier((early, late, unit))
    x_early = over_x(early)
    x_late = over_x(late)
    c_tokens = over_c(tokens[0])

    deep = 2 * rows
    from_up, from_down = up(unit), down(unit)
    y_unit = over_y(unit)
    from_up, y_unit = lax.optimization_barrier((from_up, y_unit))
    y_up = over_y(from_up)
    from_down, y_up, x_early = lax.optimization_barrier((from_down, y_up, x_early))
    y_down = over_y(from_down)
    far_ours, far_theirs = up(from_up[:deep]), down(from_down[deep:])
    far_ours, y_down = lax.optimization_barrier((far_ours, y_down))
    y_ours, y_theirs = over_y(far_ours), over_y(far_theirs)
    x_late, far_theirs, y_ours, y_theirs = lax.optimization_barrier((x_late, far_theirs, y_ours, y_theirs))
    arrays, pieces, places = [], [], []
    for value, across, from_z, kinds in (
        (unit, y_unit, z, (0, 1)),
        (from_up, y_up, z - 1, (0, 1)),
        (from_down, y_down, z + 1, (0, 1)),
        (far_ours, y_ours, z + 2, (0,)),
        (far_theirs, y_theirs, z + 2, (1,)),
    ):
        for array, from_y in ((value, y), (across, 1 - y)):
            for i, kind in enumerate(kinds):
                pieces.append((len(arrays), i * deep))
                places.append((from_y * 2 + (x ^ kind)) * chips + from_z % chips)
            arrays.append(array)
    places = jnp.stack(places).astype(jnp.int32)
    xc_early = over_c(x_early)
    xc_late = over_c(x_late)

    notes = jnp.stack([unit[2 * deep :], from_up[2 * deep :], from_down[2 * deep :], far_theirs[deep:]])
    notes = notes[:, :2, : targets.size].astype(jnp.int32)
    from_z = (z + jnp.array([0, -1, 1, 2], jnp.int32)) % chips
    own_row = from_z[:, None] == jnp.arange(chips, dtype=jnp.int32)[None]
    all_targets = jnp.sum(jnp.where(own_row[:, :, None, None], notes[:, None], 0), axis=0)
    wanted = plan_sends(all_targets.reshape(devices, *targets.shape), me, local_blocks, capacity)
    wanted = jnp.take(wanted, me ^ jnp.arange(devices, dtype=jnp.int32), axis=0)
    place = plan_receives(targets, local_blocks, capacity) ^ (me * capacity)
    core = c.astype(jnp.int32).reshape(1)

    def swap_blocks(replies):
        return [replies[0]] + [
            lax.ppermute(replies[k], ("z", "c"), [(i, i ^ k) for i in range(devices)]) for k in range(1, devices)
        ]

    def last_block(same, diff):
        edge = jnp.stack([same[-BLOCK:], diff[-BLOCK:]])
        return lax.ppermute(edge, ("z", "c"), [(i, i + 1) for i in range(devices - 1)])

    same, sent = project([tokens[0], c_tokens], arrays, pieces, places)
    diff = over_c(sent)
    x_late, sent = lax.optimization_barrier((x_late, sent))
    x_sent, xc_sent = project([x_early, x_late, xc_early, xc_late], arrays, pieces, places)
    x_same, x_diff = over_x(x_sent), over_xc(xc_sent)
    same, diff, x_sent = lax.optimization_barrier((same, diff, x_sent))
    arrived = swap_blocks(pack(wanted, core, same, diff))
    prev = last_block(same, diff)
    x_same, x_diff, prev, *arrived = lax.optimization_barrier((x_same, x_diff, prev, *arrived))
    x_prev = last_block(x_same, x_diff)
    arrived += swap_blocks(pack(wanted, core, x_same, x_diff))

    own = jnp.stack([same, diff, x_same, x_diff]).reshape(2, 2, *same.shape)
    where = jnp.stack([(me == 0).astype(jnp.int32), x, c, 1 - c]).astype(jnp.int32)
    return attend(place, where, queries[0], own, jnp.stack([prev, x_prev]), arrived)[None]


def solution(mesh):
    fsdp, seq = mesh.shape["fsdp"], mesh.shape["seq"]
    if (fsdp, seq) == (4, 8):
        mesh = Mesh(mesh.devices.reshape(2, 2, seq // 2, 2), ("y", "x", "z", "c"))
        step, fsdp, seq = local_split, ("y", "x"), ("z", "c")
    else:
        step, fsdp, seq = local_gathered, ("fsdp",), ("seq",)
    placed = (
        P(fsdp, seq, None),
        P(fsdp, seq, None),
        P((*fsdp, *seq), None),
        P((*fsdp, *seq), None),
        P(fsdp, None, seq),
    )
    return jax.shard_map(step, mesh=mesh, in_specs=placed, out_specs=P(fsdp, seq, None), check_vma=False)
```

```python
import functools
import math

import jax
import jax.numpy as jnp
from jax import lax
from jax.experimental import pallas as pl
from jax.experimental.pallas import tpu as pltpu
from jax.sharding import Mesh, PartitionSpec as P

DH = 128
KVH = 8
GROUP = 4
BLOCK = 128
TALL = GROUP * BLOCK
DIGITS = 3
EXP2_SCALE = math.log2(math.e) / math.sqrt(DH)


def plan_sends(all_targets, me, local_blocks, capacity):
    devices = all_targets.shape[0]
    targets = all_targets.reshape(devices, -1)
    heads = jnp.arange(targets.shape[1], dtype=jnp.int32) // local_blocks
    mine = targets // local_blocks == me
    rank = jnp.cumsum(mine.astype(jnp.int32), axis=1) - 1
    row = heads[None, :] * local_blocks + targets % local_blocks
    hit = mine[:, :, None] & (rank[:, :, None] == jnp.arange(capacity, dtype=jnp.int32))
    return jnp.sum(jnp.where(hit, row[:, :, None], 0), axis=1)


def plan_receives(targets, local_blocks, capacity):
    owner = targets.reshape(-1) // local_blocks
    order = jnp.arange(owner.shape[0], dtype=jnp.int32)
    same = (owner[:, None] == owner[None, :]) & (order[None, :] < order[:, None])
    return owner * capacity + jnp.sum(same.astype(jnp.int32), axis=1)


def group_rows(head, b, part):
    for i in range(TALL // BLOCK):
        group = head * GROUP + part * (TALL // BLOCK) + i
        yield i, (pl.ds(b * BLOCK, BLOCK), pl.ds(group * DH, DH))


def ahead(runs, score, finish):
    scores = score(*runs[0])
    for now, later in zip(runs, runs[1:] + [None], strict=True):
        held, scores = scores, score(*later) if later else None
        finish(*now, held)


def weighted(raised, values):
    both = jnp.concatenate([values, jnp.ones_like(values)], axis=1)
    result = jnp.dot(raised.astype(jnp.bfloat16), both, preferred_element_type=jnp.float32)
    return result[:, :DH], result[:, DH:]


def near_kernel(where_ref, q_ref, k_ref, v_ref, pk_ref, pv_ref, out_ref, log_ref):
    blocks = k_ref.shape[2] // BLOCK
    heads = k_ref.shape[3] // DH
    lane = lax.broadcasted_iota(jnp.int32, (BLOCK, DH), 1)
    logs = [jnp.zeros((BLOCK, DH), jnp.float32) for _ in range(blocks)]

    def load(ref, prev_ref, head, b):
        own, before = pl.ds(b * BLOCK, BLOCK), pl.ds((b - 1) * BLOCK, BLOCK)
        columns = pl.ds(head * DH, DH)
        prev = prev_ref[0, 0, :, columns] if b == 0 else ref[0, 0, before, columns]
        return jnp.concatenate([ref[0, 0, own, columns], prev], axis=0)

    def score(head, b, part):
        q = jnp.concatenate([q_ref[at] for _, at in group_rows(head, b, part)], axis=0)
        keys = load(k_ref, pk_ref, head, b)
        scores = lax.dot_general(q, keys, (((1,), (1,)), ((), ())), preferred_element_type=jnp.float32)
        if b == 0:
            column = lax.broadcasted_iota(jnp.int32, (1, 2 * BLOCK), 1)
            scores = jnp.where((column >= BLOCK) & (where_ref[0] == 1), -1e30, scores)
        return scores

    def finish(head, b, part, scores):
        highest = jnp.max(scores, axis=-1, keepdims=True)
        raised = jnp.exp2((scores - highest) * EXP2_SCALE)
        result, total = weighted(raised, load(v_ref, pv_ref, head, b))
        result = result * (1.0 / total)
        log = highest * EXP2_SCALE + jnp.log2(total)
        for i, at in group_rows(head, b, part):
            rows = slice(i * BLOCK, (i + 1) * BLOCK)
            out_ref[at] = result[rows]
            group, rest = head * GROUP + part * (TALL // BLOCK) + i, log[rows]
            for digit in range(DIGITS):
                rounded = rest.astype(jnp.bfloat16).astype(jnp.float32)
                logs[b] = jnp.where(lane == digit * heads * GROUP + group, rounded, logs[b])
                rest = rest - rounded

    ahead([(h, b, p) for h in range(heads) for b in range(blocks) for p in range(GROUP * BLOCK // TALL)], score, finish)
    for b in range(blocks):
        log_ref[pl.ds(b * BLOCK, BLOCK)] = logs[b].astype(jnp.bfloat16)


def far_kernel(arrays, place_ref, where_ref, q_ref, near_ref, log_ref, spread_ref, *refs):
    array_refs, (out_ref, table) = refs[:arrays], refs[arrays:]
    blocks = q_ref.shape[0] // BLOCK
    heads = q_ref.shape[1] // (GROUP * DH)
    first = pl.program_id(0) * heads * blocks

    @pl.when(pl.program_id(0) == 0)
    def _():
        for i, ref in enumerate(array_refs):
            kind, start = i // (arrays // 2), i % (arrays // 2) * ref.shape[0]
            table[kind, pl.ds(start, ref.shape[0])] = ref[...]

    logs = [
        jnp.dot(log_ref[pl.ds(b * BLOCK, BLOCK)], spread_ref[...], preferred_element_type=jnp.float32)
        for b in range(blocks)
    ]

    def load(head, b, kind):
        return table[where_ref[1] ^ kind, place_ref[first + head * blocks + b]]

    def score(head, b, part):
        q = jnp.concatenate([q_ref[at] for _, at in group_rows(head, b, part)], axis=0)
        return lax.dot_general(
            q, load(head, b, 0), (((1,), (1,)), ((), ())), preferred_element_type=jnp.float32
        )

    def finish(head, b, part, scores):
        spots = list(group_rows(head, b, part))
        log = jnp.concatenate([logs[b][:, at[1].start : at[1].start + DH] for _, at in spots], axis=0)
        near = jnp.concatenate([near_ref[at] for _, at in spots], axis=0)
        highest = jnp.maximum(jnp.max(scores, axis=-1, keepdims=True) * EXP2_SCALE, log)
        far, total = weighted(jnp.exp2(scores * EXP2_SCALE - highest), load(head, b, 1))
        share = jnp.exp2(log - highest)
        result = ((near * share + far) * (1.0 / (share + total))).astype(jnp.bfloat16)
        for i, at in spots:
            out_ref[at] = result[i * BLOCK : (i + 1) * BLOCK]

    ahead([(h, b, p) for h in range(heads) for b in range(blocks) for p in range(GROUP * BLOCK // TALL)], score, finish)


def attend(place, where, queries, own, prev, arrived):
    tokens, columns = queries.shape
    blocks = tokens // BLOCK
    step = 4
    width = step * GROUP * DH
    steps = own.shape[3] // (step * DH)

    def kv_spec(rows, kind, at):
        def index(h, where):
            return (where[1] ^ kind, (h // steps) ^ where[at], 0, h % steps)

        return pl.BlockSpec((1, 1, rows, step * DH), index)

    near, logs = pl.pallas_call(
        near_kernel,
        grid_spec=pltpu.PrefetchScalarGridSpec(
            num_scalar_prefetch=1,
            grid=(KVH // step,),
            in_specs=[
                pl.BlockSpec((tokens, width), lambda h, where: (0, h)),
                kv_spec(tokens, 0, 2),
                kv_spec(tokens, 1, 2),
                kv_spec(BLOCK, 0, 3),
                kv_spec(BLOCK, 1, 3),
            ],
            out_specs=[
                pl.BlockSpec((tokens, width), lambda h, where: (0, h)),
                pl.BlockSpec((tokens, DH), lambda h, where: (0, h)),
            ],
        ),
        out_shape=[
            jax.ShapeDtypeStruct(queries.shape, jnp.float32),
            jax.ShapeDtypeStruct((tokens, KVH // step * DH), jnp.bfloat16),
        ],
        cost_estimate=pl.CostEstimate(
            flops=8 * tokens * columns * BLOCK, bytes_accessed=8 * tokens * columns, transcendentals=2 * tokens * columns
        ),
        compiler_params=pltpu.CompilerParams(vmem_limit_bytes=14 * 1024 * 1024),
    )(where, queries, own, own, prev, prev)
    q_spec = pl.BlockSpec((tokens, width), lambda h, place, where: (0, h))
    digit = jnp.arange(DH)[:, None] - jnp.arange(width)[None] // DH
    groups = step * GROUP
    spread = ((digit >= 0) & (digit % groups == 0) & (digit < DIGITS * groups)).astype(jnp.bfloat16)
    return pl.pallas_call(
        functools.partial(far_kernel, len(arrived)),
        grid_spec=pltpu.PrefetchScalarGridSpec(
            num_scalar_prefetch=2,
            grid=(KVH // step,),
            in_specs=[
                q_spec,
                q_spec,
                pl.BlockSpec((tokens, DH), lambda h, place, where: (0, h)),
                pl.BlockSpec(spread.shape, lambda h, place, where: (0, 0)),
                *[pl.BlockSpec(array.shape, lambda h, place, where: (0, 0, 0)) for array in arrived],
            ],
            out_specs=q_spec,
            scratch_shapes=[
                pltpu.VMEM((2, sum(array.shape[0] for array in arrived) // 2, BLOCK, DH), jnp.bfloat16),
            ],
        ),
        out_shape=jax.ShapeDtypeStruct(queries.shape, jnp.bfloat16),
        cost_estimate=pl.CostEstimate(
            flops=4 * tokens * columns * BLOCK, bytes_accessed=8 * tokens * columns, transcendentals=tokens * columns
        ),
        compiler_params=pltpu.CompilerParams(vmem_limit_bytes=(10 << 20) + 4 * sum(array.nbytes for array in arrived)),
    )(place, where, queries, near, logs, spread, *arrived)


def local_gathered(tokens, queries, key_weight, value_weight, sorted_blocks):
    local_blocks = tokens.shape[1] // BLOCK
    devices = lax.axis_size("seq")
    me = lax.axis_index("seq")
    capacity = (KVH * local_blocks + devices - 1) // devices
    targets = sorted_blocks[0]
    wanted = plan_sends(lax.all_gather(targets, "seq", axis=0), me, local_blocks, capacity)
    place = plan_receives(targets, local_blocks, capacity)
    weights = lax.all_gather(
        jnp.concatenate([key_weight, value_weight], axis=1), ("fsdp", "seq"), axis=0, tiled=True
    )
    packed = jnp.dot(tokens[0], weights, preferred_element_type=jnp.float32).astype(jnp.bfloat16)
    own = jnp.stack([packed[:, : KVH * DH], packed[:, KVH * DH :]])[:, None]
    prev = lax.ppermute(own[:, :, -BLOCK:], "seq", [(i, i + 1) for i in range(devices - 1)])
    table = own.reshape(2, local_blocks, BLOCK, KVH, DH).transpose(3, 1, 0, 2, 4)
    replies = jnp.take(table.reshape(-1, 2, BLOCK, DH), wanted.reshape(-1), axis=0)
    arrived = lax.all_to_all(replies, "seq", split_axis=0, concat_axis=0, tiled=True)
    zero = jnp.zeros_like(me)
    where = jnp.stack([(me == 0).astype(jnp.int32), zero, zero, zero])
    return attend(place, where, queries[0], own, prev, [arrived[:, 0], arrived[:, 1]])[None]


def project_kernel(runs, arrays, pieces, place_ref, *refs):
    token_refs, array_refs = refs[:runs], refs[runs : runs + arrays]
    out_refs, (tokens, weights, token_sems, piece_sems) = refs[runs + arrays : -4], refs[-4:]
    depth = weights.shape[0] // len(pieces)
    tall = out_refs[0].shape[0] // 2
    arrivals, copies, start = [], [], 0
    for i, (array, first) in enumerate(pieces):
        rows = pl.ds(pl.multiple_of(place_ref[i] * depth, depth), depth)
        source = array_refs[array].at[pl.ds(first, depth)]
        arrivals.append(pltpu.make_async_copy(source, weights.at[rows], piece_sems.at[i]))
    for i, ref in enumerate(token_refs):
        rows = ref.shape[0]
        copy = pltpu.make_async_copy(ref, tokens.at[pl.ds(start, rows)], token_sems.at[i])
        copies.append((copy, start // tall))
        start += rows
    for copy in arrivals:
        copy.start()
    for copy, _ in copies:
        copy.start()
    for copy in arrivals:
        copy.wait()
    for i in range(2 * len(out_refs)):
        for copy, of in copies:
            if of == i:
                copy.wait()
        product = jnp.dot(tokens[i * tall : (i + 1) * tall], weights[...], preferred_element_type=jnp.float32)
        out_refs[i // 2][i % 2 * tall : (i % 2 + 1) * tall] = product.astype(jnp.bfloat16)


def project(token_runs, arrays, pieces, places):
    tokens = sum(run.shape[0] for run in token_runs)
    depth, width = token_runs[0].shape[1], arrays[0].shape[1]
    anywhere = pl.BlockSpec(memory_space=pl.ANY)
    return pl.pallas_call(
        functools.partial(project_kernel, len(token_runs), len(arrays), pieces),
        grid_spec=pltpu.PrefetchScalarGridSpec(
            num_scalar_prefetch=1,
            grid=(),
            in_specs=[anywhere] * (len(token_runs) + len(arrays)),
            out_specs=[pl.BlockSpec(memory_space=pltpu.VMEM)] * 2,
            scratch_shapes=[
                pltpu.VMEM((tokens, depth), jnp.bfloat16),
                pltpu.VMEM((depth, width), jnp.bfloat16),
                pltpu.SemaphoreType.DMA((len(token_runs),)),
                pltpu.SemaphoreType.DMA((len(pieces),)),
            ],
        ),
        out_shape=[jax.ShapeDtypeStruct((tokens // 2, width), jnp.bfloat16)] * 2,
        cost_estimate=pl.CostEstimate(
            flops=2 * tokens * depth * width, bytes_accessed=2 * (tokens + width) * depth, transcendentals=0
        ),
        compiler_params=pltpu.CompilerParams(vmem_limit_bytes=14 * 1024 * 1024),
    )(places, *token_runs, *arrays)


def pack_kernel(row_ref, part_ref, same_ref, diff_ref, *refs):
    out_refs, table = refs[:-1], refs[-1]
    heads = table.shape[2] // DH
    blocks = table.shape[1] // BLOCK
    capacity = out_refs[0].shape[0]
    table[0] = same_ref[...]
    table[1] = diff_ref[...]
    for i in range(row_ref.shape[0]):
        head, block = row_ref[i] // blocks, row_ref[i] % blocks
        out_refs[i // capacity][i % capacity] = table[
            (head // heads) ^ part_ref[0],
            pl.ds(pl.multiple_of(block * BLOCK, BLOCK), BLOCK),
            pl.ds(pl.multiple_of((head % heads) * DH, DH), DH),
        ]


def pack(wanted, part, same, diff):
    devices, capacity = wanted.shape
    return pl.pallas_call(
        pack_kernel,
        grid_spec=pltpu.PrefetchScalarGridSpec(
            num_scalar_prefetch=2,
            grid=(),
            in_specs=[pl.BlockSpec(memory_space=pltpu.VMEM)] * 2,
            out_specs=[pl.BlockSpec(memory_space=pltpu.VMEM)] * devices,
            scratch_shapes=[pltpu.VMEM((2, *same.shape), jnp.bfloat16)],
        ),
        out_shape=[jax.ShapeDtypeStruct((capacity, BLOCK, DH), jnp.bfloat16)] * devices,
        compiler_params=pltpu.CompilerParams(vmem_limit_bytes=6 * 1024 * 1024),
    )(wanted.reshape(-1), part, same, diff)


def local_split(tokens, queries, key_weight, value_weight, sorted_blocks):
    y, x, z, c = [lax.axis_index(name) for name in ("y", "x", "z", "c")]
    chips = lax.axis_size("z")
    devices = 2 * chips
    me = 2 * z + c
    local_blocks = tokens.shape[1] // BLOCK
    capacity = (KVH * local_blocks + devices - 1) // devices
    half = KVH * DH // 2
    targets = sorted_blocks[0]

    near = jnp.where(x == 0, key_weight, value_weight)
    away = jnp.where(x == 0, value_weight, key_weight)

    def part(weight, core):
        return lax.dynamic_slice_in_dim(weight, core * half, half, 1)

    def along(axis, step):
        count = lax.axis_size(axis)
        return lambda value: lax.ppermute(value, axis, [(i, (i + step) % count) for i in range(count)])

    over_x, over_y, over_c, up, down = along("x", 1), along("y", 1), along("c", 1), along("z", 1), along("z", -1)

    def over_xc(value):
        return lax.ppermute(value, ("x", "c"), [(i, 3 - i) for i in range(4)])

    def by_core(same_core, other_core):
        pair = jnp.stack([same_core, other_core])
        return jnp.where(c == 0, pair, pair[::-1])

    rows = key_weight.shape[0]
    notes = jnp.zeros((16, half), jnp.bfloat16).at[0, : targets.size].set(targets.reshape(-1).astype(jnp.bfloat16))
    from_x, from_xc = over_x(part(away, c)), over_xc(part(away, 1 - c))
    from_c = over_c(jnp.concatenate([part(near, 1 - c), notes]))
    ours = by_core(part(near, c), from_c[:rows]).reshape(-1, half)
    theirs = by_core(from_x, from_xc).reshape(-1, half)
    notes = by_core(notes[:1], from_c[rows : rows + 1]).reshape(-1, half)
    unit = jnp.concatenate([ours, theirs, notes, jnp.zeros((14, half), jnp.bfloat16)])

    whole, unit = lax.optimization_barrier((tokens[0], unit))
    x_tokens = over_x(whole)
    c_tokens = over_c(tokens[0])

    deep = 2 * rows
    from_up = up(unit)
    y_unit = over_y(unit)
    from_up, y_unit, again = lax.optimization_barrier((from_up, y_unit, unit))
    from_down = down(again)
    y_up = over_y(from_up)
    from_down, y_up = lax.optimization_barrier((from_down, y_up))
    y_down = over_y(from_down)
    far_ours, far_theirs = up(from_up[:deep]), down(from_down[deep:])
    far_ours, y_down = lax.optimization_barrier((far_ours, y_down))
    y_ours, y_theirs = over_y(far_ours), over_y(far_theirs)
    x_tokens, far_theirs, y_ours, y_theirs = lax.optimization_barrier((x_tokens, far_theirs, y_ours, y_theirs))
    arrays, pieces, places = [], [], []
    for value, across, from_z, kinds in (
        (unit, y_unit, z, (0, 1)),
        (from_up, y_up, z - 1, (0, 1)),
        (from_down, y_down, z + 1, (0, 1)),
        (far_ours, y_ours, z + 2, (0,)),
        (far_theirs, y_theirs, z + 2, (1,)),
    ):
        for array, from_y in ((value, y), (across, 1 - y)):
            for i, kind in enumerate(kinds):
                pieces.append((len(arrays), i * deep))
                places.append((from_y * 2 + (x ^ kind)) * chips + from_z % chips)
            arrays.append(array)
    places = jnp.stack(places).astype(jnp.int32)
    xc_tokens = over_c(x_tokens)

    notes = jnp.stack([unit[2 * deep :], from_up[2 * deep :], from_down[2 * deep :], far_theirs[deep:]])
    notes = notes[:, :2, : targets.size].astype(jnp.int32)
    from_z = (z + jnp.array([0, -1, 1, 2], jnp.int32)) % chips
    own_row = from_z[:, None] == jnp.arange(chips, dtype=jnp.int32)[None]
    all_targets = jnp.sum(jnp.where(own_row[:, :, None, None], notes[:, None], 0), axis=0)
    wanted = plan_sends(all_targets.reshape(devices, *targets.shape), me, local_blocks, capacity)
    wanted = jnp.take(wanted, me ^ jnp.arange(devices, dtype=jnp.int32), axis=0)
    place = plan_receives(targets, local_blocks, capacity) ^ (me * capacity)
    core = c.astype(jnp.int32).reshape(1)

    def swap_blocks(replies):
        return [replies[0]] + [
            lax.ppermute(replies[k], ("z", "c"), [(i, i ^ k) for i in range(devices)]) for k in range(1, devices)
        ]

    same, sent = project([tokens[0], c_tokens], arrays, pieces, places)
    diff = over_c(sent)
    x_tokens, sent = lax.optimization_barrier((x_tokens, sent))
    x_sent, xc_sent = project([x_tokens, xc_tokens], arrays, pieces, places)
    x_same, x_diff = over_x(x_sent), over_xc(xc_sent)
    same, diff, x_sent = lax.optimization_barrier((same, diff, x_sent))
    arrived = swap_blocks(pack(wanted, core, same, diff))
    x_same, x_diff, *arrived = lax.optimization_barrier((x_same, x_diff, *arrived))
    arrived += swap_blocks(pack(wanted, core, x_same, x_diff))

    own = jnp.stack([same, diff, x_same, x_diff]).reshape(2, 2, *same.shape)
    prev = lax.ppermute(own[:, :, -BLOCK:], ("z", "c"), [(i, i + 1) for i in range(devices - 1)])
    where = jnp.stack([(me == 0).astype(jnp.int32), x, c, 1 - c]).astype(jnp.int32)
    return attend(place, where, queries[0], own, prev, arrived)[None]


def solution(mesh):
    fsdp, seq = mesh.shape["fsdp"], mesh.shape["seq"]
    if (fsdp, seq) == (4, 8):
        mesh = Mesh(mesh.devices.reshape(2, 2, seq // 2, 2), ("y", "x", "z", "c"))
        step, fsdp, seq = local_split, ("y", "x"), ("z", "c")
    else:
        step, fsdp, seq = local_gathered, ("fsdp",), ("seq",)
    placed = (
        P(fsdp, seq, None),
        P(fsdp, seq, None),
        P((*fsdp, *seq), None),
        P((*fsdp, *seq), None),
        P(fsdp, None, seq),
    )
    return jax.shard_map(step, mesh=mesh, in_specs=placed, out_specs=P(fsdp, seq, None), check_vma=False)
```

```python
import functools
import math

import jax
import jax.numpy as jnp
from jax import lax
from jax.experimental import pallas as pl
from jax.experimental.pallas import tpu as pltpu
from jax.sharding import Mesh, PartitionSpec as P

DH = 128
KVH = 8
GROUP = 4
BLOCK = 128
TALL = GROUP * BLOCK
DIGITS = 3
EXP2_SCALE = math.log2(math.e) / math.sqrt(DH)


def plan_sends(all_targets, me, local_blocks, capacity):
    devices = all_targets.shape[0]
    targets = all_targets.reshape(devices, -1)
    heads = jnp.arange(targets.shape[1], dtype=jnp.int32) // local_blocks
    mine = targets // local_blocks == me
    rank = jnp.cumsum(mine.astype(jnp.int32), axis=1) - 1
    row = heads[None, :] * local_blocks + targets % local_blocks
    hit = mine[:, :, None] & (rank[:, :, None] == jnp.arange(capacity, dtype=jnp.int32))
    return jnp.sum(jnp.where(hit, row[:, :, None], 0), axis=1)


def plan_receives(targets, local_blocks, capacity):
    owner = targets.reshape(-1) // local_blocks
    order = jnp.arange(owner.shape[0], dtype=jnp.int32)
    same = (owner[:, None] == owner[None, :]) & (order[None, :] < order[:, None])
    return owner * capacity + jnp.sum(same.astype(jnp.int32), axis=1)


def group_rows(head, b, part):
    for i in range(TALL // BLOCK):
        group = head * GROUP + part * (TALL // BLOCK) + i
        yield i, (pl.ds(b * BLOCK, BLOCK), pl.ds(group * DH, DH))


def ahead(runs, score, finish):
    scores = score(*runs[0])
    for now, later in zip(runs, runs[1:] + [None], strict=True):
        held, scores = scores, score(*later) if later else None
        finish(*now, held)


def weighted(raised, values):
    both = jnp.concatenate([values, jnp.ones_like(values)], axis=1)
    result = jnp.dot(raised.astype(jnp.bfloat16), both, preferred_element_type=jnp.float32)
    return result[:, :DH], result[:, DH:]


def near_kernel(where_ref, q_ref, k_ref, v_ref, pk_ref, pv_ref, out_ref, log_ref):
    blocks = k_ref.shape[2] // BLOCK
    heads = k_ref.shape[3] // DH
    lane = lax.broadcasted_iota(jnp.int32, (BLOCK, DH), 1)
    logs = [jnp.zeros((BLOCK, DH), jnp.float32) for _ in range(blocks)]

    def load(ref, prev_ref, head, b):
        own, before = pl.ds(b * BLOCK, BLOCK), pl.ds((b - 1) * BLOCK, BLOCK)
        columns = pl.ds(head * DH, DH)
        prev = prev_ref[0, 0, :, columns] if b == 0 else ref[0, 0, before, columns]
        return jnp.concatenate([ref[0, 0, own, columns], prev], axis=0)

    def score(head, b, part):
        q = jnp.concatenate([q_ref[at] for _, at in group_rows(head, b, part)], axis=0)
        keys = load(k_ref, pk_ref, head, b)
        scores = lax.dot_general(q, keys, (((1,), (1,)), ((), ())), preferred_element_type=jnp.float32)
        if b == 0:
            column = lax.broadcasted_iota(jnp.int32, (1, 2 * BLOCK), 1)
            scores = jnp.where((column >= BLOCK) & (where_ref[0] == 1), -1e30, scores)
        return scores

    def finish(head, b, part, scores):
        highest = jnp.max(scores, axis=-1, keepdims=True)
        raised = jnp.exp2((scores - highest) * EXP2_SCALE)
        result, total = weighted(raised, load(v_ref, pv_ref, head, b))
        result = result * (1.0 / total)
        log = highest * EXP2_SCALE + jnp.log2(total)
        for i, at in group_rows(head, b, part):
            rows = slice(i * BLOCK, (i + 1) * BLOCK)
            out_ref[at] = result[rows]
            group, rest = head * GROUP + part * (TALL // BLOCK) + i, log[rows]
            for digit in range(DIGITS):
                rounded = rest.astype(jnp.bfloat16).astype(jnp.float32)
                logs[b] = jnp.where(lane == digit * heads * GROUP + group, rounded, logs[b])
                rest = rest - rounded

    ahead([(h, b, p) for h in range(heads) for b in range(blocks) for p in range(GROUP * BLOCK // TALL)], score, finish)
    for b in range(blocks):
        log_ref[pl.ds(b * BLOCK, BLOCK)] = logs[b].astype(jnp.bfloat16)


def far_kernel(arrays, place_ref, where_ref, q_ref, near_ref, log_ref, spread_ref, *refs):
    array_refs, (out_ref, table) = refs[:arrays], refs[arrays:]
    blocks = q_ref.shape[0] // BLOCK
    heads = q_ref.shape[1] // (GROUP * DH)
    first = pl.program_id(0) * heads * blocks

    @pl.when(pl.program_id(0) == 0)
    def _():
        for i, ref in enumerate(array_refs):
            kind, start = i // (arrays // 2), i % (arrays // 2) * ref.shape[0]
            table[kind, pl.ds(start, ref.shape[0])] = ref[...]

    logs = [
        jnp.dot(log_ref[pl.ds(b * BLOCK, BLOCK)], spread_ref[...], preferred_element_type=jnp.float32)
        for b in range(blocks)
    ]

    def load(head, b, kind):
        return table[where_ref[1] ^ kind, place_ref[first + head * blocks + b]]

    def score(head, b, part):
        q = jnp.concatenate([q_ref[at] for _, at in group_rows(head, b, part)], axis=0)
        return lax.dot_general(
            q, load(head, b, 0), (((1,), (1,)), ((), ())), preferred_element_type=jnp.float32
        )

    def finish(head, b, part, scores):
        spots = list(group_rows(head, b, part))
        log = jnp.concatenate([logs[b][:, at[1].start : at[1].start + DH] for _, at in spots], axis=0)
        near = jnp.concatenate([near_ref[at] for _, at in spots], axis=0)
        highest = jnp.maximum(jnp.max(scores, axis=-1, keepdims=True) * EXP2_SCALE, log)
        far, total = weighted(jnp.exp2(scores * EXP2_SCALE - highest), load(head, b, 1))
        share = jnp.exp2(log - highest)
        result = ((near * share + far) * (1.0 / (share + total))).astype(jnp.bfloat16)
        for i, at in spots:
            out_ref[at] = result[i * BLOCK : (i + 1) * BLOCK]

    ahead([(h, b, p) for h in range(heads) for b in range(blocks) for p in range(GROUP * BLOCK // TALL)], score, finish)


def attend(place, where, queries, own, prev, arrived):
    tokens, columns = queries.shape
    blocks = tokens // BLOCK
    step = 4
    width = step * GROUP * DH
    steps = own.shape[3] // (step * DH)

    def kv_spec(rows, kind, at):
        def index(h, where):
            return (where[1] ^ kind, (h // steps) ^ where[at], 0, h % steps)

        return pl.BlockSpec((1, 1, rows, step * DH), index)

    near, logs = pl.pallas_call(
        near_kernel,
        grid_spec=pltpu.PrefetchScalarGridSpec(
            num_scalar_prefetch=1,
            grid=(KVH // step,),
            in_specs=[
                pl.BlockSpec((tokens, width), lambda h, where: (0, h)),
                kv_spec(tokens, 0, 2),
                kv_spec(tokens, 1, 2),
                kv_spec(BLOCK, 0, 3),
                kv_spec(BLOCK, 1, 3),
            ],
            out_specs=[
                pl.BlockSpec((tokens, width), lambda h, where: (0, h)),
                pl.BlockSpec((tokens, DH), lambda h, where: (0, h)),
            ],
        ),
        out_shape=[
            jax.ShapeDtypeStruct(queries.shape, jnp.float32),
            jax.ShapeDtypeStruct((tokens, KVH // step * DH), jnp.bfloat16),
        ],
        cost_estimate=pl.CostEstimate(
            flops=8 * tokens * columns * BLOCK, bytes_accessed=8 * tokens * columns, transcendentals=2 * tokens * columns
        ),
        compiler_params=pltpu.CompilerParams(vmem_limit_bytes=14 * 1024 * 1024),
    )(where, queries, own, own, prev, prev)
    q_spec = pl.BlockSpec((tokens, width), lambda h, place, where: (0, h))
    digit = jnp.arange(DH)[:, None] - jnp.arange(width)[None] // DH
    groups = step * GROUP
    spread = ((digit >= 0) & (digit % groups == 0) & (digit < DIGITS * groups)).astype(jnp.bfloat16)
    return pl.pallas_call(
        functools.partial(far_kernel, len(arrived)),
        grid_spec=pltpu.PrefetchScalarGridSpec(
            num_scalar_prefetch=2,
            grid=(KVH // step,),
            in_specs=[
                q_spec,
                q_spec,
                pl.BlockSpec((tokens, DH), lambda h, place, where: (0, h)),
                pl.BlockSpec(spread.shape, lambda h, place, where: (0, 0)),
                *[pl.BlockSpec(array.shape, lambda h, place, where: (0, 0, 0)) for array in arrived],
            ],
            out_specs=q_spec,
            scratch_shapes=[
                pltpu.VMEM((2, sum(array.shape[0] for array in arrived) // 2, BLOCK, DH), jnp.bfloat16),
            ],
        ),
        out_shape=jax.ShapeDtypeStruct(queries.shape, jnp.bfloat16),
        cost_estimate=pl.CostEstimate(
            flops=4 * tokens * columns * BLOCK, bytes_accessed=8 * tokens * columns, transcendentals=tokens * columns
        ),
        compiler_params=pltpu.CompilerParams(vmem_limit_bytes=(10 << 20) + 4 * sum(array.nbytes for array in arrived)),
    )(place, where, queries, near, logs, spread, *arrived)


def local_gathered(tokens, queries, key_weight, value_weight, sorted_blocks):
    local_blocks = tokens.shape[1] // BLOCK
    devices = lax.axis_size("seq")
    me = lax.axis_index("seq")
    capacity = (KVH * local_blocks + devices - 1) // devices
    targets = sorted_blocks[0]
    wanted = plan_sends(lax.all_gather(targets, "seq", axis=0), me, local_blocks, capacity)
    place = plan_receives(targets, local_blocks, capacity)
    weights = lax.all_gather(
        jnp.concatenate([key_weight, value_weight], axis=1), ("fsdp", "seq"), axis=0, tiled=True
    )
    packed = jnp.dot(tokens[0], weights, preferred_element_type=jnp.float32).astype(jnp.bfloat16)
    own = jnp.stack([packed[:, : KVH * DH], packed[:, KVH * DH :]])[:, None]
    prev = lax.ppermute(own[:, :, -BLOCK:], "seq", [(i, i + 1) for i in range(devices - 1)])
    table = own.reshape(2, local_blocks, BLOCK, KVH, DH).transpose(3, 1, 0, 2, 4)
    replies = jnp.take(table.reshape(-1, 2, BLOCK, DH), wanted.reshape(-1), axis=0)
    arrived = lax.all_to_all(replies, "seq", split_axis=0, concat_axis=0, tiled=True)
    zero = jnp.zeros_like(me)
    where = jnp.stack([(me == 0).astype(jnp.int32), zero, zero, zero])
    return attend(place, where, queries[0], own, prev, [arrived[:, 0], arrived[:, 1]])[None]


def project_kernel(runs, arrays, pieces, place_ref, *refs):
    token_refs, array_refs = refs[:runs], refs[runs : runs + arrays]
    out_refs, (tokens, weights, token_sems, piece_sems) = refs[runs + arrays : -4], refs[-4:]
    depth = weights.shape[0] // len(pieces)
    tall = out_refs[0].shape[0] // 2
    arrivals, copies, start = [], [], 0
    for i, (array, first) in enumerate(pieces):
        rows = pl.ds(pl.multiple_of(place_ref[i] * depth, depth), depth)
        source = array_refs[array].at[pl.ds(first, depth)]
        arrivals.append(pltpu.make_async_copy(source, weights.at[rows], piece_sems.at[i]))
    for i, ref in enumerate(token_refs):
        rows = ref.shape[0]
        copy = pltpu.make_async_copy(ref, tokens.at[pl.ds(start, rows)], token_sems.at[i])
        copies.append((copy, start // tall))
        start += rows
    for copy in arrivals:
        copy.start()
    for copy, _ in copies:
        copy.start()
    for copy in arrivals:
        copy.wait()
    for i in range(2 * len(out_refs)):
        for copy, of in copies:
            if of == i:
                copy.wait()
        product = jnp.dot(tokens[i * tall : (i + 1) * tall], weights[...], preferred_element_type=jnp.float32)
        out_refs[i // 2][i % 2 * tall : (i % 2 + 1) * tall] = product.astype(jnp.bfloat16)


def project(token_runs, arrays, pieces, places):
    tokens = sum(run.shape[0] for run in token_runs)
    depth, width = token_runs[0].shape[1], arrays[0].shape[1]
    anywhere = pl.BlockSpec(memory_space=pl.ANY)
    return pl.pallas_call(
        functools.partial(project_kernel, len(token_runs), len(arrays), pieces),
        grid_spec=pltpu.PrefetchScalarGridSpec(
            num_scalar_prefetch=1,
            grid=(),
            in_specs=[anywhere] * (len(token_runs) + len(arrays)),
            out_specs=[pl.BlockSpec(memory_space=pltpu.VMEM)] * 2,
            scratch_shapes=[
                pltpu.VMEM((tokens, depth), jnp.bfloat16),
                pltpu.VMEM((depth, width), jnp.bfloat16),
                pltpu.SemaphoreType.DMA((len(token_runs),)),
                pltpu.SemaphoreType.DMA((len(pieces),)),
            ],
        ),
        out_shape=[jax.ShapeDtypeStruct((tokens // 2, width), jnp.bfloat16)] * 2,
        cost_estimate=pl.CostEstimate(
            flops=2 * tokens * depth * width, bytes_accessed=2 * (tokens + width) * depth, transcendentals=0
        ),
        compiler_params=pltpu.CompilerParams(vmem_limit_bytes=14 * 1024 * 1024),
    )(places, *token_runs, *arrays)


def pack_kernel(row_ref, part_ref, same_ref, diff_ref, *refs):
    out_refs, table = refs[:-1], refs[-1]
    heads = table.shape[2] // DH
    blocks = table.shape[1] // BLOCK
    capacity = out_refs[0].shape[0]
    table[0] = same_ref[...]
    table[1] = diff_ref[...]
    for i in range(row_ref.shape[0]):
        head, block = row_ref[i] // blocks, row_ref[i] % blocks
        out_refs[i // capacity][i % capacity] = table[
            (head // heads) ^ part_ref[0],
            pl.ds(pl.multiple_of(block * BLOCK, BLOCK), BLOCK),
            pl.ds(pl.multiple_of((head % heads) * DH, DH), DH),
        ]


def pack(wanted, part, same, diff):
    devices, capacity = wanted.shape
    return pl.pallas_call(
        pack_kernel,
        grid_spec=pltpu.PrefetchScalarGridSpec(
            num_scalar_prefetch=2,
            grid=(),
            in_specs=[pl.BlockSpec(memory_space=pltpu.VMEM)] * 2,
            out_specs=[pl.BlockSpec(memory_space=pltpu.VMEM)] * devices,
            scratch_shapes=[pltpu.VMEM((2, *same.shape), jnp.bfloat16)],
        ),
        out_shape=[jax.ShapeDtypeStruct((capacity, BLOCK, DH), jnp.bfloat16)] * devices,
        compiler_params=pltpu.CompilerParams(vmem_limit_bytes=6 * 1024 * 1024),
    )(wanted.reshape(-1), part, same, diff)


def local_split(tokens, queries, key_weight, value_weight, sorted_blocks):
    y, x, z, c = [lax.axis_index(name) for name in ("y", "x", "z", "c")]
    chips = lax.axis_size("z")
    devices = 2 * chips
    me = 2 * z + c
    local_blocks = tokens.shape[1] // BLOCK
    capacity = (KVH * local_blocks + devices - 1) // devices
    half = KVH * DH // 2
    targets = sorted_blocks[0]

    near = jnp.where(x == 0, key_weight, value_weight)
    away = jnp.where(x == 0, value_weight, key_weight)

    def part(weight, core):
        return lax.dynamic_slice_in_dim(weight, core * half, half, 1)

    def along(axis, step):
        count = lax.axis_size(axis)
        return lambda value: lax.ppermute(value, axis, [(i, (i + step) % count) for i in range(count)])

    over_x, over_y, over_c, up, down = along("x", 1), along("y", 1), along("c", 1), along("z", 1), along("z", -1)

    def over_xc(value):
        return lax.ppermute(value, ("x", "c"), [(i, 3 - i) for i in range(4)])

    def by_core(same_core, other_core):
        pair = jnp.stack([same_core, other_core])
        return jnp.where(c == 0, pair, pair[::-1])

    rows = key_weight.shape[0]
    notes = jnp.zeros((16, half), jnp.bfloat16).at[0, : targets.size].set(targets.reshape(-1).astype(jnp.bfloat16))
    from_x, from_xc = over_x(part(away, c)), over_xc(part(away, 1 - c))
    from_c = over_c(jnp.concatenate([part(near, 1 - c), notes]))
    ours = by_core(part(near, c), from_c[:rows]).reshape(-1, half)
    theirs = by_core(from_x, from_xc).reshape(-1, half)
    notes = by_core(notes[:1], from_c[rows : rows + 1]).reshape(-1, half)
    unit = jnp.concatenate([ours, theirs, notes, jnp.zeros((14, half), jnp.bfloat16)])

    whole, unit = lax.optimization_barrier((tokens[0], unit))
    x_tokens = over_x(whole)
    c_tokens = over_c(tokens[0])

    deep = 2 * rows
    from_up = up(unit)
    y_unit = over_y(unit)
    from_up, y_unit, again = lax.optimization_barrier((from_up, y_unit, unit))
    from_down = down(again)
    y_up = over_y(from_up)
    from_down, y_up = lax.optimization_barrier((from_down, y_up))
    y_down = over_y(from_down)
    far_ours, far_theirs = up(from_up[:deep]), down(from_down[deep:])
    far_ours, y_down = lax.optimization_barrier((far_ours, y_down))
    y_ours, y_theirs = over_y(far_ours), over_y(far_theirs)
    x_tokens, far_theirs, y_ours, y_theirs = lax.optimization_barrier((x_tokens, far_theirs, y_ours, y_theirs))
    arrays, pieces, places = [], [], []
    for value, across, from_z, kinds in (
        (unit, y_unit, z, (0, 1)),
        (from_up, y_up, z - 1, (0, 1)),
        (from_down, y_down, z + 1, (0, 1)),
        (far_ours, y_ours, z + 2, (0,)),
        (far_theirs, y_theirs, z + 2, (1,)),
    ):
        for array, from_y in ((value, y), (across, 1 - y)):
            for i, kind in enumerate(kinds):
                pieces.append((len(arrays), i * deep))
                places.append((from_y * 2 + (x ^ kind)) * chips + from_z % chips)
            arrays.append(array)
    places = jnp.stack(places).astype(jnp.int32)
    xc_tokens = over_c(x_tokens)

    notes = jnp.stack([unit[2 * deep :], from_up[2 * deep :], from_down[2 * deep :], far_theirs[deep:]])
    notes = notes[:, :2, : targets.size].astype(jnp.int32)
    from_z = (z + jnp.array([0, -1, 1, 2], jnp.int32)) % chips
    own_row = from_z[:, None] == jnp.arange(chips, dtype=jnp.int32)[None]
    all_targets = jnp.sum(jnp.where(own_row[:, :, None, None], notes[:, None], 0), axis=0)
    wanted = plan_sends(all_targets.reshape(devices, *targets.shape), me, local_blocks, capacity)
    wanted = jnp.take(wanted, me ^ jnp.arange(devices, dtype=jnp.int32), axis=0)
    place = plan_receives(targets, local_blocks, capacity) ^ (me * capacity)
    core = c.astype(jnp.int32).reshape(1)

    def swap_blocks(replies):
        swapped = {
            k: lax.ppermute(replies[k], ("z", "c"), [(i, i ^ k) for i in range(devices)])
            for k in reversed(range(1, devices))
        }
        return [replies[0]] + [swapped[k] for k in range(1, devices)]

    same, sent = project([tokens[0], c_tokens], arrays, pieces, places)
    diff = over_c(sent)
    x_tokens, sent = lax.optimization_barrier((x_tokens, sent))
    x_sent, xc_sent = project([x_tokens, xc_tokens], arrays, pieces, places)
    x_same, x_diff = over_x(x_sent), over_xc(xc_sent)
    same, diff, x_sent = lax.optimization_barrier((same, diff, x_sent))
    arrived = swap_blocks(pack(wanted, core, same, diff))
    x_same, x_diff, *arrived = lax.optimization_barrier((x_same, x_diff, *arrived))
    arrived += swap_blocks(pack(wanted, core, x_same, x_diff))

    own = jnp.stack([same, diff, x_same, x_diff]).reshape(2, 2, *same.shape)
    prev = lax.ppermute(own[:, :, -BLOCK:], ("z", "c"), [(i, i + 1) for i in range(devices - 1)])
    where = jnp.stack([(me == 0).astype(jnp.int32), x, c, 1 - c]).astype(jnp.int32)
    return attend(place, where, queries[0], own, prev, arrived)[None]


def solution(mesh):
    fsdp, seq = mesh.shape["fsdp"], mesh.shape["seq"]
    if (fsdp, seq) == (4, 8):
        mesh = Mesh(mesh.devices.reshape(2, 2, seq // 2, 2), ("y", "x", "z", "c"))
        step, fsdp, seq = local_split, ("y", "x"), ("z", "c")
    else:
        step, fsdp, seq = local_gathered, ("fsdp",), ("seq",)
    placed = (
        P(fsdp, seq, None),
        P(fsdp, seq, None),
        P((*fsdp, *seq), None),
        P((*fsdp, *seq), None),
        P(fsdp, None, seq),
    )
    return jax.shard_map(step, mesh=mesh, in_specs=placed, out_specs=P(fsdp, seq, None), check_vma=False)
```
